32 devices in a mesh: section: 2 (over x), lat: 4 (over z), tp: 4 (over y, core).
Axes of the slice: x: 2, y: 2, z: 4, core: 2. Of those that a mesh axis runs over, the one named last changes fastest.
Arguments:
- initial_field: bfloat16 [2, 8, 12, 48, 192], P(None, 'tp', 'lat'), may hold values from -6 to 6
- first_gain: bfloat16 [2, 192], P('section'), may hold values from 0.25 to 1.75
- first_shift: bfloat16 [2, 192], P('section'), may hold values from -1.75 to 1.75
- qkv_weight: bfloat16 [2, 192, 576], P('section', None, 'tp'), may hold values from -0.4375 to 0.4375
- qkv_bias: bfloat16 [2, 576], P('section', 'tp'), may hold values from -1.75 to 1.75
- proj_weight: bfloat16 [2, 192, 192], P('section', None, 'tp'), may hold values from -0.4375 to 0.4375
- proj_bias: bfloat16 [2, 192], P('section', 'tp'), may hold values from -1.75 to 1.75
- second_gain: bfloat16 [2, 192], P('section'), may hold values from 0.25 to 1.75
- second_shift: bfloat16 [2, 192], P('section'), may hold values from -1.75 to 1.75
- expand_weight: bfloat16 [2, 192, 768], P('section', None, 'tp'), may hold values from -0.4375 to 0.4375
- expand_bias: bfloat16 [2, 768], P('section', 'tp'), may hold values from -1.75 to 1.75
- reduce_weight: bfloat16 [2, 768, 192], P('section', 'tp'), may hold values from -0.21875 to 0.21875
- reduce_bias: bfloat16 [2, 192], P('section', 'tp'), may hold values from -1.75 to 1.75
- earth_bias: float32 [2, 4, 4, 6, 1656], P('section', 'tp', 'lat'), may hold values from -4 to 340
Outputs:
- predicted_states: bfloat16 [2, 2, 8, 12, 48, 192], P('section', None, 'tp', 'lat')
The draws below stay inside these ranges and needn't reach their ends.
All inputs are finite; a program needn't handle non-finite values.
Results may differ from the reference program's by a relative error of at most 0.018.
Values may be sent and summed in bfloat16 or wider, within the bound.
A program may use at most 64 MiB of HBM per device.

```python
import jax
import jax.numpy as jnp
import numpy as np
from jax import lax

C = 192
HEADS = 6
LEV = 8
LON = 48
MICRO = 2
WZ = 2
WH = 6
WW = 12
LAT = 12
MLP_WIDTH = 768
HALF_BIAS_COUNT = 1656


def draw_earth_bias(key, part):
    half_rows = WH // 2
    shape = (2, LEV // WZ, LAT // half_rows, HEADS, HALF_BIAS_COUNT)
    noise = jnp.clip(jax.random.normal(jax.random.fold_in(key, 11), shape, jnp.float32), -4.0, 4.0)
    return noise


def shard_levels(key, shape, cuts, smallest, largest):
    level = 1.0
    for dim, blocks in cuts:
        heights = jax.random.uniform(jax.random.fold_in(jax.random.fold_in(key, 6), dim), (blocks,), jnp.float32, smallest / len(cuts), largest / len(cuts))
        level = level * jnp.repeat(jnp.exp(heights), shape[dim] // blocks).reshape((-1,) + (1,) * (len(shape) - 1 - dim))
    return level


def centred(own_key, dims, scale, most, cuts=(), dtype=jnp.bfloat16):
    factor_of = shard_levels(own_key, dims, cuts, -0.22, 0.18) if cuts else 1.0
    values = jax.random.normal(own_key, dims, jnp.float32) * scale * factor_of
    return jnp.minimum(jnp.maximum(values, -most), most).astype(dtype)


def setup_inputs(seed: int = 0) -> dict:
    key_list = jax.random.split(jax.random.key(seed), 15)
    return {
        "initial_field": centred(key_list[0], (MICRO, LEV, LAT, LON, C), 1.0, 6.0, ((1, 4), (2, 4))),
        "first_gain": jnp.clip(1.0 + 0.15 * jax.random.normal(key_list[1], (2, C), jnp.float32), 0.25, 1.75).astype(jnp.bfloat16),
        "first_shift": centred(key_list[2], (2, C), 0.3, 1.75, ((0, 2),)),
        "qkv_weight": centred(key_list[3], (2, C, 3 * C), C ** -0.5, 0.4375, ((0, 2), (2, 4))),
        "qkv_bias": centred(key_list[4], (2, 3 * C), 0.3, 1.75, ((0, 2), (1, 4))),
        "proj_weight": centred(key_list[5], (2, C, C), C ** -0.5, 0.4375, ((0, 2), (2, 4))),
        "proj_bias": centred(key_list[6], (2, C), 0.3, 1.75, ((0, 2), (1, 4))),
        "second_gain": jnp.clip(1.0 + 0.15 * jax.random.normal(key_list[7], (2, C), jnp.float32), 0.25, 1.75).astype(jnp.bfloat16),
        "second_shift": centred(key_list[8], (2, C), 0.3, 1.75, ((0, 2),)),
        "expand_weight": centred(key_list[9], (2, C, MLP_WIDTH), C ** -0.5, 0.4375, ((0, 2), (2, 4))),
        "expand_bias": centred(key_list[10], (2, MLP_WIDTH), 0.3, 1.75, ((0, 2), (1, 4))),
        "reduce_weight": centred(key_list[11], (2, MLP_WIDTH, C), MLP_WIDTH ** -0.5, 0.21875, ((0, 2), (1, 4))),
        "reduce_bias": centred(key_list[12], (2, C), 0.3, 1.75, ((0, 2), (1, 4))),
        "earth_bias": draw_earth_bias(jax.random.fold_in(key_list[14], 71), 0),
    }


epsilon = 1e-05

def bias_entries():
    half_rows = WH // 2
    query_pos = np.arange(WZ * half_rows * WW)
    attended_location = np.arange(WZ * WH * WW)
    query_level = query_pos // (half_rows * WW)
    query_row = query_pos // WW % half_rows
    query_col = query_pos % WW
    key_level = attended_location // (WH * WW)
    key_row = attended_location // WW % WH
    key_column_index = attended_location % WW
    table_items = (((query_level[:, None] * WZ + key_level[None, :]) * half_rows + query_row[:, None]) * WH + key_row[None, :]) * (2 * WW - 1) + (query_col[:, None] - key_column_index[None, :] + WW - 1)
    return table_items.astype(np.int32)

def layer_norm(values, gain, offset):
    floats = values.astype(jnp.float32)
    middle_point = lax.optimization_barrier(jnp.mean(floats, axis=-1, keepdims=True))
    spread = lax.optimization_barrier(jnp.mean((floats - middle_point) ** 2, axis=-1, keepdims=True))
    return (floats - middle_point) * lax.rsqrt(spread + epsilon) * gain.astype(jnp.float32) + offset.astype(jnp.float32)

def to_windows(grid, band_rows):
    levels, lat_rows, lon_cols, feats = grid.shape
    shaped = grid.reshape(levels // WZ, WZ, lat_rows // band_rows, band_rows, lon_cols // WW, WW, feats)
    shaped = shaped.transpose(2, 0, 4, 1, 3, 5, 6)
    return shaped.reshape(lat_rows // band_rows, levels // WZ, lon_cols // WW, WZ * band_rows * WW, feats)

def from_windows(blocks, levels, lat_rows, lon_cols):
    band_rows = WH // 2
    feats = blocks.shape[-1]
    shaped = blocks.reshape(lat_rows // band_rows, levels // WZ, lon_cols // WW, WZ, band_rows, WW, feats)
    shaped = shaped.transpose(1, 3, 0, 4, 2, 5, 6)
    return shaped.reshape(levels, lat_rows, lon_cols, feats)

def earth_block(grid, model_index, params, bias_table):
    first_gain, first_shift, qkv_weight, qkv_bias, proj_weight, proj_bias, second_gain, second_shift, expand_weight, expand_bias, reduce_weight, reduce_bias = params
    levels, lat_rows, lon_cols, width = grid.shape
    heads = bias_table.shape[-2]
    head_size = width // heads
    scale = 1.0 / float(np.sqrt(head_size))
    normed = layer_norm(grid, first_gain[model_index], first_shift[model_index]).astype(jnp.bfloat16)
    flat = normed.reshape(-1, width)
    mixed = (jnp.dot(flat, qkv_weight[model_index], preferred_element_type=jnp.float32) + qkv_bias[model_index].astype(jnp.float32)).astype(jnp.bfloat16)
    mixed = mixed.reshape(levels, lat_rows, lon_cols, 3 * width)
    query_rows = to_windows(mixed[..., :width], WH // 2)
    keyvals = jnp.repeat(to_windows(mixed[..., width:], WH), 2, axis=0)
    table_items = jnp.asarray(bias_entries())
    tables = jnp.transpose(bias_table, (1, 0, 2, 3))

    def attend(pieces):
        query_block, keyval_block, table_block = pieces
        level_wins, meridian_slabs, query_count, feats = query_block.shape
        key_count = keyval_block.shape[2]
        bias_block = jnp.take(table_block, table_items, axis=2)
        query_heads = query_block.astype(jnp.float32).reshape(level_wins, meridian_slabs, query_count, heads, head_size)
        key_heads = keyval_block[..., :width].astype(jnp.float32).reshape(level_wins, meridian_slabs, key_count, heads, head_size)
        value_heads = keyval_block[..., width:].astype(jnp.float32).reshape(level_wins, meridian_slabs, key_count, heads, head_size)
        scores = jnp.einsum('lwqhd,lwkhd->lwhqk', query_heads, key_heads) * scale + bias_block[:, None]
        probs = jax.nn.softmax(scores, axis=-1).astype(jnp.bfloat16)
        attended = jnp.einsum('lwhqk,lwkhd->lwqhd', probs.astype(jnp.float32), value_heads)
        return attended.reshape(level_wins, meridian_slabs, query_count, width).astype(jnp.bfloat16)
    attended = lax.map(attend, (query_rows, keyvals, tables))
    merged = from_windows(attended, levels, lat_rows, lon_cols).reshape(-1, width)
    branch = jnp.dot(merged, proj_weight[model_index], preferred_element_type=jnp.float32) + proj_bias[model_index].astype(jnp.float32)
    middle = (grid.reshape(-1, width).astype(jnp.float32) + branch).astype(jnp.bfloat16)
    normed_two = layer_norm(middle, second_gain[model_index], second_shift[model_index]).astype(jnp.bfloat16)
    hidden = jax.nn.gelu(jnp.dot(normed_two, expand_weight[model_index], preferred_element_type=jnp.float32) + expand_bias[model_index].astype(jnp.float32), approximate=False).astype(jnp.bfloat16)
    result = (middle.astype(jnp.float32) + jnp.dot(hidden, reduce_weight[model_index], preferred_element_type=jnp.float32) + reduce_bias[model_index].astype(jnp.float32)).astype(jnp.bfloat16)
    return result.reshape(levels, lat_rows, lon_cols, width)

def reference(initial_field, first_gain, first_shift, qkv_weight, qkv_bias, proj_weight, proj_bias, second_gain, second_shift, expand_weight, expand_bias, reduce_weight, reduce_bias, earth_bias):
    params = (first_gain, first_shift, qkv_weight, qkv_bias, proj_weight, proj_bias, second_gain, second_shift, expand_weight, expand_bias, reduce_weight, reduce_bias)
    daily_lead_times = []
    quarter_lead_times = []
    for turn_index in range(MICRO):
        first_out = earth_block(initial_field[turn_index], 0, params, earth_bias[0])
        second_out = earth_block(first_out, 1, params, earth_bias[1])
        daily_lead_times.append(first_out)
        quarter_lead_times.append(second_out)
    return jnp.stack([jnp.stack(daily_lead_times), jnp.stack(quarter_lead_times)])
```

```python
import functools

import jax
import jax.numpy as jnp
import numpy as np
from jax import lax
from jax.experimental import pallas as pl
from jax.experimental.pallas import tpu as pltpu
from jax.sharding import PartitionSpec as P

WZ = 2
WH = 6
WW = 12
HALF = WH // 2
GROUP = WZ * HALF
EPS = 1e-05
MESH = pl.DeviceIdType.MESH
F32 = jnp.float32
BF16 = jnp.bfloat16
NT = (((1,), (1,)), ((), ()))


def mm(a, b):
    return jnp.dot(a, b, preferred_element_type=F32)


def mm_nt(a, b):
    return lax.dot_general(a, b, NT, preferred_element_type=F32)


def layer_norm(values, gain, shift):
    mean = jnp.mean(values, axis=-1, keepdims=True)
    centred = values - mean
    spread = jnp.mean(centred * centred, axis=-1, keepdims=True)
    return centred * lax.rsqrt(spread + EPS) * gain + shift


def kernel(
    tp, micro, heads, slabs,
    x_ref, g1_ref, s1_ref, qw_ref, qb_ref, pw_ref, pb_ref, g2_ref, s2_ref,
    ew_ref, eb_ref, rw_ref, rb_ref, table_ref,
    out_ref,
    qkv, proj, expand, reduce, near, inbuf, outp, perm, unperm,
    own_n, near_n, att_n, table, bias,
    w_send, w_recv, f_send, f_recv, o_send, o_recv,
):
    me = lax.axis_index("tp")
    lat = lax.axis_index("lat")
    section = lax.axis_index("section")
    pair = lat + 1 - 2 * lax.rem(lat, 2)
    other = 1 - section
    cells, width = x_ref.shape[1:]
    wide = own_n.shape[1]
    half_cells = cells // slabs
    head_size = width // heads
    q_part, p_part = qw_ref.shape[1], pw_ref.shape[1]
    e_rows = width + 16

    barrier = pltpu.get_barrier_semaphore()
    for k in range(1, tp):
        pl.semaphore_signal(barrier, inc=1, device_id={"tp": lax.rem(me + k, tp)}, device_id_type=MESH)
    pl.semaphore_signal(barrier, inc=1, device_id={"lat": pair}, device_id_type=MESH)
    pl.semaphore_signal(barrier, inc=1, device_id={"section": other}, device_id_type=MESH)
    pl.semaphore_signal(barrier, inc=1, device_id={"section": other, "lat": pair}, device_id_type=MESH)

    tail = lax.broadcasted_iota(jnp.int32, (wide - width, q_part), 0)
    q_own = jnp.concatenate(
        [qw_ref[...].astype(F32), jnp.where(tail == 0, qb_ref[...].astype(F32), 0.0)], axis=0)
    q_rows = pl.ds(pl.multiple_of(me * q_part, 16), q_part)
    qkv[q_rows, :] = q_own.T.astype(BF16)
    tail = lax.broadcasted_iota(jnp.int32, (wide - width, p_part), 0)
    p_own = jnp.concatenate(
        [pw_ref[...].astype(F32),
         jnp.where(tail == 0, pb_ref[...].astype(F32), jnp.where(tail == 1, rb_ref[...].astype(F32), 0.0))],
        axis=0)
    p_rows = pl.ds(pl.multiple_of(me * p_part, 16), p_part)
    proj[p_rows, :] = p_own.T.astype(BF16)
    expand[:, e_rows:, :] = jnp.zeros_like(expand[:, e_rows:, :])
    expand[me, :width, :] = ew_ref[...]
    tail = lax.broadcasted_iota(jnp.int32, (16, width), 0)
    expand[me, width:e_rows, :] = jnp.where(tail == 0, eb_ref[...].astype(F32), 0.0).astype(BF16)
    reduce[me] = rw_ref[...]

    pl.semaphore_wait(barrier, tp + 2)

    def weight_copy(kind, k):
        ref = (
            qkv.at[q_rows, :],
            proj.at[p_rows, :],
            expand.at[me, pl.ds(0, e_rows), :],
            reduce.at[me],
        )[kind]
        return pltpu.make_async_remote_copy(
            src_ref=ref, dst_ref=ref, send_sem=w_send.at[kind, k - 1], recv_sem=w_recv.at[kind, k - 1],
            device_id={"tp": lax.rem(me + k, tp)}, device_id_type=MESH)

    def field_copy():
        return pltpu.make_async_remote_copy(
            src_ref=x_ref, dst_ref=near, send_sem=f_send, recv_sem=f_recv,
            device_id={"lat": pair}, device_id_type=MESH)

    def state_copy(t, which):
        target = {"section": other} if which == 0 else {"section": other, "lat": pair}
        return pltpu.make_async_remote_copy(
            src_ref=outp.at[t], dst_ref=inbuf.at[t, which], send_sem=o_send.at[t, which],
            recv_sem=o_recv.at[t, which], device_id=target, device_id_type=MESH)

    for k in range(1, tp):
        weight_copy(0, k).start()

    @pl.when(section == 0)
    def _():
        field_copy().start()

    for kind in (1, 2, 3):
        for k in range(1, tp):
            weight_copy(kind, k).start()

    stretch = cells // GROUP

    def target_of(j):
        a = sum((j >= stretch * k).astype(jnp.int32) for k in range(1, GROUP))
        return (j - stretch * a) * GROUP + a

    rows = lax.broadcasted_iota(jnp.int32, (cells, cells), 0)
    cols = lax.broadcasted_iota(jnp.int32, (cells, cells), 1)
    perm[...] = (rows == target_of(cols)).astype(F32).astype(BF16)
    unperm[...] = (cols == target_of(rows)).astype(F32).astype(BF16)
    lanes = lax.broadcasted_iota(jnp.int32, (cells, wide), 1)
    ones = (lanes == width).astype(F32).astype(BF16)
    own_n[...] = ones
    near_n[...] = ones
    att_n[...] = ones

    @pl.when(section == 0)
    def _():
        for t in range(micro):
            inbuf[t, 0] = mm(perm[...], x_ref[t]).astype(BF16)

    table[...] = jnp.zeros_like(table)
    span = WH * (2 * WW - 1)
    for zq in range(WZ):
        for zk in range(WZ):
            for r in range(HALF):
                off = ((zq * WZ + zk) * HALF + r) * span
                piece = table_ref[:, off:off + span]
                for h in range(heads):
                    row = h * GROUP + zq * HALF + r
                    table[row:row + 1, zk * 256:zk * 256 + span] = piece[h:h + 1]
    c = lax.broadcasted_iota(jnp.int32, (table.shape[1], 2 * half_cells), 1)
    far = (c >= half_cells).astype(jnp.int32)
    c = c - half_cells * far
    wk = sum((c >= GROUP * k).astype(jnp.int32) for k in range(1, WW))
    zr = c - GROUP * wk
    zk = (zr >= HALF).astype(jnp.int32)
    band = lax.rem(lat, 2)
    hk = zr - HALF * zk + HALF * (band + far - 2 * band * far)
    place = zk * 256 + hk * (2 * WW - 1) + WW - 1 - wk
    pick = (lax.broadcasted_iota(jnp.int32, place.shape, 0) == place).astype(F32).astype(BF16)
    full = table[...]
    lines = full.shape[0]
    for wq in range(WW):
        turned = full if wq == 0 else pltpu.roll(full, full.shape[1] - wq, 1)
        first = turned.astype(BF16)
        rest = turned - first.astype(F32)
        second = rest.astype(BF16)
        third = (rest - second.astype(F32)).astype(BF16)
        parts = mm(jnp.concatenate([first, second, third], axis=0), pick)
        total = parts[:lines] + parts[lines:2 * lines] + parts[2 * lines:]
        for h in range(heads):
            at = h * half_cells + wq * GROUP
            bias[at:at + GROUP, :] = total[h * GROUP:(h + 1) * GROUP]

    @pl.when(section == 0)
    def _():
        field_copy().wait_recv()
        for t in range(micro):
            inbuf[t, 1] = mm(perm[...], near[t]).astype(BF16)

    scale = 1.0 / float(np.sqrt(head_size))
    lane_head = lax.broadcasted_iota(jnp.int32, (half_cells, width), 1)
    in_head = [(lane_head >= h * head_size) & (lane_head < (h + 1) * head_size) for h in range(heads)]

    def weights_here(t, kind):
        @pl.when(t == 0)
        def _():
            for k in range(1, tp):
                weight_copy(kind, k).wait_recv()

    def turn(t, carry):
        @pl.when(section == 1)
        def _():
            state_copy(t, 0).wait_recv()
            state_copy(t, 1).wait_recv()

        g1, s1 = g1_ref[...].astype(F32), s1_ref[...].astype(F32)
        g2, s2 = g2_ref[...].astype(F32), s2_ref[...].astype(F32)
        grid = inbuf[t, 0].astype(F32)
        own_n[:, :width] = layer_norm(grid, g1, s1).astype(BF16)
        near_n[:, :width] = layer_norm(inbuf[t, 1].astype(F32), g1, s1).astype(BF16)
        weights_here(t, 0)
        q = mm_nt(own_n[...], qkv[:width, :])
        k_own = mm_nt(own_n[...], qkv[width:2 * width, :])
        v_own = mm_nt(own_n[...], qkv[2 * width:, :])
        k_near = mm_nt(near_n[...], qkv[width:2 * width, :])
        v_near = mm_nt(near_n[...], qkv[2 * width:, :])
        attended = []
        for s in range(slabs):
            cut = slice(s * half_cells, (s + 1) * half_cells)
            keys = jnp.concatenate([k_own[cut], k_near[cut]], axis=0).astype(BF16)
            vals = jnp.concatenate([v_own[cut], v_near[cut]], axis=0).astype(BF16)
            stack = jnp.concatenate([jnp.where(m, q[cut], 0.0) for m in in_head], axis=0).astype(BF16)
            scores = mm_nt(stack, keys) * scale + bias[...]
            e = jnp.exp(scores - jnp.max(scores, axis=-1, keepdims=True))
            probs = (e * (1.0 / jnp.sum(e, axis=-1, keepdims=True))).astype(BF16)
            mixed = mm(probs, vals)
            total = jnp.zeros((half_cells, width), F32)
            for h, m in enumerate(in_head):
                total = jnp.where(m, mixed[h * half_cells:(h + 1) * half_cells], total)
            attended.append(total)
        att_n[:, :width] = jnp.concatenate(attended, axis=0).astype(BF16)
        weights_here(t, 1)
        middle = (grid + mm_nt(att_n[...], proj[...])).astype(BF16).astype(F32)
        pick_row = (lax.broadcasted_iota(jnp.int32, (16, wide), 1) == width + 1).astype(F32).astype(BF16)
        shift_out = mm_nt(pick_row, proj[...])[:1]
        own_n[:, :width] = layer_norm(middle, g2, s2).astype(BF16)
        weights_here(t, 2)
        result = middle + shift_out
        hidden = []
        for i in range(tp):
            pre = mm(own_n[...], expand[i])
            hidden.append((0.5 * pre * (1.0 + lax.erf(pre * float(np.sqrt(0.5))))).astype(BF16))
        weights_here(t, 3)
        for i in range(tp):
            result = result + mm(hidden[i], reduce[i])
        outp[t] = result.astype(BF16)

        @pl.when(section == 0)
        def _():
            state_copy(t, 0).start()
            state_copy(t, 1).start()

        out_ref[t] = mm(unperm[...], outp[t]).astype(BF16)
        return carry

    lax.fori_loop(0, micro, turn, 0)

    for kind in range(4):
        for k in range(1, tp):
            weight_copy(kind, k).wait_send()

    @pl.when(section == 0)
    def _():
        field_copy().wait_send()
        for t in range(micro):
            state_copy(t, 0).wait_send()
            state_copy(t, 1).wait_send()


def on_device(
    initial_field, first_gain, first_shift, qkv_weight, qkv_bias, proj_weight, proj_bias,
    second_gain, second_shift, expand_weight, expand_bias, reduce_weight, reduce_bias, earth_bias,
):
    tp = lax.axis_size("tp")
    micro, levels, lat_rows, lon, width = initial_field.shape
    cells = levels * lat_rows * lon
    heads, entries = earth_bias.shape[-2:]
    slabs = lon // WW
    half_cells = cells // slabs
    wide = -(-(width + 2) // 128) * 128
    lines = -(-heads * GROUP // 16) * 16
    vmem = pl.BlockSpec(memory_space=pltpu.VMEM)
    dma = pltpu.SemaphoreType.DMA
    out = pl.pallas_call(
        functools.partial(kernel, tp, micro, heads, slabs),
        out_shape=jax.ShapeDtypeStruct((micro, cells, width), BF16),
        in_specs=[vmem] * 14,
        out_specs=vmem,
        scratch_shapes=[
            pltpu.VMEM((3 * width, wide), BF16),
            pltpu.VMEM((width, wide), BF16),
            pltpu.VMEM((tp, wide, width), BF16),
            pltpu.VMEM((tp, width, width), BF16),
            pltpu.VMEM((micro, cells, width), BF16),
            pltpu.VMEM((micro, 2, cells, width), BF16),
            pltpu.VMEM((micro, cells, width), BF16),
            pltpu.VMEM((cells, cells), BF16),
            pltpu.VMEM((cells, cells), BF16),
            pltpu.VMEM((cells, wide), BF16),
            pltpu.VMEM((cells, wide), BF16),
            pltpu.VMEM((cells, wide), BF16),
            pltpu.VMEM((lines, 512), F32),
            pltpu.VMEM((heads * half_cells, 2 * half_cells), F32),
            dma((4, tp - 1)),
            dma((4, tp - 1)),
            dma,
            dma,
            dma((micro, 2)),
            dma((micro, 2)),
        ],
        compiler_params=pltpu.CompilerParams(
            collective_id=0, has_side_effects=True, vmem_limit_bytes=40 * 1024 * 1024),
    )(
        initial_field.reshape(micro, cells, width), first_gain, first_shift, qkv_weight[0], qkv_bias,
        proj_weight[0], proj_bias, second_gain, second_shift, expand_weight[0], expand_bias,
        reduce_weight[0], reduce_bias, earth_bias.reshape(heads, entries),
    )
    return out.reshape(1, micro, levels, lat_rows, lon, width)


def solution(mesh):
    return jax.shard_map(
        on_device,
        mesh=mesh,
        in_specs=(
            P(None, "tp", "lat", None, None),
            P("section", None),
            P("section", None),
            P("section", None, "tp"),
            P("section", "tp"),
            P("section", None, "tp"),
            P("section", "tp"),
            P("section", None),
            P("section", None),
            P("section", None, "tp"),
            P("section", "tp"),
            P("section", "tp", None),
            P("section", "tp"),
            P("section", "tp", "lat", None, None),
        ),
        out_specs=P("section", None, "tp", "lat", None, None),
        check_vma=False,
    )
```

```python
import functools

import jax
import jax.numpy as jnp
import numpy as np
from jax import lax
from jax.experimental import pallas as pl
from jax.experimental.pallas import tpu as pltpu
from jax.sharding import PartitionSpec as P

WZ = 2
WH = 6
WW = 12
HALF = WH // 2
GROUP = WZ * HALF
EPS = 1e-05
MESH = pl.DeviceIdType.MESH
F32 = jnp.float32
BF16 = jnp.bfloat16
NT = (((1,), (1,)), ((), ()))


def mm(a, b):
    return jnp.dot(a, b, preferred_element_type=F32)


def mm_nt(a, b):
    return lax.dot_general(a, b, NT, preferred_element_type=F32)


def layer_norm(values, gain, shift):
    mean = jnp.mean(values, axis=-1, keepdims=True)
    centred = values - mean
    spread = jnp.mean(centred * centred, axis=-1, keepdims=True)
    return centred * lax.rsqrt(spread + EPS) * gain + shift


def kernel(
    tp, micro, heads, slabs,
    x_in, g1_in, s1_in, qw_in, qb_in, pw_in, pb_in, g2_in, s2_in,
    ew_in, eb_in, rw_in, rb_in, table_in,
    out_ref,
    x_ref, g1_ref, s1_ref, qw_ref, qb_ref, pw_ref, pb_ref, g2_ref, s2_ref,
    ew_ref, eb_ref, rb_ref, table_ref,
    qkv, proj, expand, reduce, near, inbuf, outp, perm, unperm,
    own_n, near_n, att_n, table, bias,
    l_sem, w_send, w_recv, f_send, f_recv, o_send, o_recv,
):
    me = lax.axis_index("tp")
    lat = lax.axis_index("lat")
    section = lax.axis_index("section")
    pair = lat + 1 - 2 * lax.rem(lat, 2)
    other = 1 - section
    cells, width = x_ref.shape[1:]
    wide = own_n.shape[1]
    half_cells = cells // slabs
    head_size = width // heads
    q_part, p_part = qw_ref.shape[0], pw_ref.shape[0]
    e_rows = width + 16
    core_peer = me + 1 - 2 * lax.rem(me, 2)
    chip_peer = lax.rem(me + tp // 2, tp)

    barrier = pltpu.get_barrier_semaphore()
    pl.semaphore_signal(barrier, inc=1, device_id={"tp": core_peer}, device_id_type=MESH)
    pl.semaphore_signal(barrier, inc=1, device_id={"tp": chip_peer}, device_id_type=MESH)
    pl.semaphore_signal(barrier, inc=1, device_id={"lat": pair}, device_id_type=MESH)
    pl.semaphore_signal(barrier, inc=1, device_id={"section": other}, device_id_type=MESH)
    pl.semaphore_signal(barrier, inc=1, device_id={"section": other, "lat": pair}, device_id_type=MESH)

    loads = [
        pltpu.make_async_copy(source, target, l_sem.at[n])
        for n, (source, target) in enumerate((
            (qw_in, qw_ref), (qb_in, qb_ref), (pw_in, pw_ref), (pb_in, pb_ref), (rb_in, rb_ref),
            (ew_in, ew_ref), (eb_in, eb_ref), (rw_in, reduce.at[me]), (x_in, x_ref), (table_in, table_ref),
            (g1_in, g1_ref), (s1_in, s1_ref), (g2_in, g2_ref), (s2_in, s2_ref),
        ))
    ]
    for load in loads:
        load.start()

    expand[:, e_rows:, :] = jnp.zeros_like(expand[:, e_rows:, :])

    def owner_rows(owner, part):
        return pl.ds(pl.multiple_of(owner * part, 16), part)

    for load in loads[:5]:
        load.wait()
    tail = lax.broadcasted_iota(jnp.int32, (wide - width, q_part), 0)
    q_tail = jnp.where(tail == 0, qb_ref[...].astype(F32), 0.0).T
    qkv[owner_rows(me, q_part), :] = jnp.concatenate(
        [qw_ref[...].astype(F32), q_tail], axis=1).astype(BF16)
    tail = lax.broadcasted_iota(jnp.int32, (wide - width, p_part), 0)
    p_tail = jnp.where(
        tail == 0, pb_ref[...].astype(F32), jnp.where(tail == 1, rb_ref[...].astype(F32), 0.0)).T
    proj[owner_rows(me, p_part), :] = jnp.concatenate(
        [pw_ref[...].astype(F32), p_tail], axis=1).astype(BF16)
    for load in loads[5:8]:
        load.wait()
    expand[me, :width, :] = ew_ref[...]
    tail = lax.broadcasted_iota(jnp.int32, (16, width), 0)
    expand[me, width:e_rows, :] = jnp.where(tail == 0, eb_ref[...].astype(F32), 0.0).astype(BF16)

    pl.semaphore_wait(barrier, 5)

    def weight_copy(kind, way):
        owner = chip_peer if way == 2 else me
        ref = (
            lambda: qkv.at[owner_rows(owner, q_part), :],
            lambda: proj.at[owner_rows(owner, p_part), :],
            lambda: expand.at[owner, pl.ds(0, e_rows), :],
            lambda: reduce.at[owner],
        )[kind]()
        return pltpu.make_async_remote_copy(
            src_ref=ref, dst_ref=ref, send_sem=w_send.at[kind, way], recv_sem=w_recv.at[kind, way],
            device_id={"tp": chip_peer if way == 1 else core_peer}, device_id_type=MESH)

    def hand_on(kind):
        weight_copy(kind, 1).wait_recv()
        weight_copy(kind, 2).start()

    def field_copy():
        return pltpu.make_async_remote_copy(
            src_ref=x_in, dst_ref=near, send_sem=f_send, recv_sem=f_recv,
            device_id={"lat": pair}, device_id_type=MESH)

    chunks = o_send.shape[2]
    chunk = cells // chunks

    def state_copy(t, which, part):
        rows = pl.ds(part * chunk, chunk)
        target = {"section": other} if which == 0 else {"section": other, "lat": pair}
        return pltpu.make_async_remote_copy(
            src_ref=outp.at[t, rows], dst_ref=inbuf.at[t, which, rows], send_sem=o_send.at[t, which, part],
            recv_sem=o_recv.at[t, which, part], device_id=target, device_id_type=MESH)

    def state_forward(t, part):
        rows = pl.ds(part * chunk, chunk)
        return pltpu.make_async_remote_copy(
            src_ref=inbuf.at[t, 0, rows], dst_ref=inbuf.at[t, 1, rows], send_sem=o_send.at[t, 1, part],
            recv_sem=o_recv.at[t, 1, part], device_id={"lat": pair}, device_id_type=MESH)

    for way in (0, 1):
        weight_copy(0, way).start()

    @pl.when(section == 0)
    def _():
        field_copy().start()

    for kind in (1, 2, 3):
        for way in (0, 1):
            weight_copy(kind, way).start()
    for load in loads[8:]:
        load.wait()

    stretch = cells // GROUP
    step = -(-65536 // GROUP)
    line = lax.broadcasted_iota(jnp.int32, (1, cells), 1)
    level_row = sum((line >= stretch * k).astype(jnp.int32) for k in range(1, GROUP))
    forth = (line - stretch * level_row) * GROUP + level_row
    column = lax.shift_right_logical(line * step, 16)
    back = (line - GROUP * column) * stretch + column
    rows = lax.broadcasted_iota(jnp.int32, (cells, cells), 0)
    perm[...] = (rows == forth).astype(F32).astype(BF16)
    unperm[...] = (rows == back).astype(F32).astype(BF16)
    lanes = lax.broadcasted_iota(jnp.int32, (cells, wide), 1)
    ones = (lanes == width).astype(F32).astype(BF16)
    own_n[...] = ones
    near_n[...] = ones
    att_n[...] = ones

    @pl.when(section == 0)
    def _():
        for t in range(micro):
            inbuf[t, 0] = mm(perm[...], x_ref[t]).astype(BF16)

    table[...] = jnp.zeros_like(table)
    span = WH * (2 * WW - 1)
    for zq in range(WZ):
        for zk in range(WZ):
            for r in range(HALF):
                off = ((zq * WZ + zk) * HALF + r) * span
                piece = table_ref[:, 0, off:off + span]
                for h in range(heads):
                    row = h * GROUP + zq * HALF + r
                    table[row:row + 1, zk * span:(zk + 1) * span] = piece[h:h + 1]
    c = lax.broadcasted_iota(jnp.int32, (1, 2 * half_cells), 1)
    far = (c >= half_cells).astype(jnp.int32)
    c = c - half_cells * far
    wk = sum((c >= GROUP * k).astype(jnp.int32) for k in range(1, WW))
    zr = c - GROUP * wk
    zk = (zr >= HALF).astype(jnp.int32)
    band = lax.rem(lat, 2)
    hk = zr - HALF * zk + HALF * (band + far - 2 * band * far)
    place = zk * span + hk * (2 * WW - 1) + WW - 1 - wk
    pick = (lax.broadcasted_iota(jnp.int32, (table.shape[1], 2 * half_cells), 0) == place).astype(F32).astype(BF16)
    full = table[...]
    lines = full.shape[0]
    for wq in range(WW):
        turned = full if wq == 0 else pltpu.roll(full, full.shape[1] - wq, 1)
        first = turned.astype(BF16)
        rest = turned - first.astype(F32)
        second = rest.astype(BF16)
        third = (rest - second.astype(F32)).astype(BF16)
        parts = mm(
            jnp.concatenate([p.astype(F32) for p in (first, second, third)], axis=0).astype(BF16), pick)
        total = parts[:lines] + parts[lines:2 * lines] + parts[2 * lines:]
        for h in range(heads):
            at = h * half_cells + wq * GROUP
            bias[at:at + GROUP, :] = total[h * GROUP:(h + 1) * GROUP]

    hand_on(0)
    hand_on(1)

    @pl.when(section == 0)
    def _():
        field_copy().wait_recv()
        for t in range(micro):
            inbuf[t, 1] = mm(perm[...], near[t]).astype(BF16)

    scale = 1.0 / float(np.sqrt(head_size))
    lane_head = lax.broadcasted_iota(jnp.int32, (half_cells, width), 1)
    in_head = [(lane_head >= h * head_size) & (lane_head < (h + 1) * head_size) for h in range(heads)]

    def weights_here(t, kind):
        @pl.when(t == 0)
        def _():
            weight_copy(kind, 0).wait_recv()
            weight_copy(kind, 2).wait_recv()

    def turn(t, carry):
        @pl.when(section == 1)
        def _():
            for part in range(chunks):
                state_copy(t, 0, part).wait_recv()
                if part < chunks - 1:
                    state_forward(t, part).start()
            for part in range(chunks):
                state_copy(t, 1, part).wait_recv()

        g1, s1 = g1_ref[...].astype(F32), s1_ref[...].astype(F32)
        g2, s2 = g2_ref[...].astype(F32), s2_ref[...].astype(F32)
        grid = inbuf[t, 0].astype(F32)
        own_n[:, :width] = layer_norm(grid, g1, s1).astype(BF16)
        near_n[:, :width] = layer_norm(inbuf[t, 1].astype(F32), g1, s1).astype(BF16)
        weights_here(t, 0)
        q = mm_nt(own_n[...], qkv[:width, :])
        k_own = mm_nt(own_n[...], qkv[width:2 * width, :])
        v_own = mm_nt(own_n[...], qkv[2 * width:, :])
        k_near = mm_nt(near_n[...], qkv[width:2 * width, :])
        v_near = mm_nt(near_n[...], qkv[2 * width:, :])
        attended = []
        for s in range(slabs):
            cut = slice(s * half_cells, (s + 1) * half_cells)
            keys = jnp.concatenate([k_own[cut], k_near[cut]], axis=0).astype(BF16)
            vals = jnp.concatenate([v_own[cut], v_near[cut]], axis=0).astype(BF16)
            stack = jnp.concatenate([jnp.where(m, q[cut], 0.0) for m in in_head], axis=0).astype(BF16)
            scores = mm_nt(stack, keys) * scale + bias[...]
            e = jnp.exp(scores - jnp.max(scores, axis=-1, keepdims=True))
            probs = (e * (1.0 / jnp.sum(e, axis=-1, keepdims=True))).astype(BF16)
            mixed = mm(probs, vals)
            total = jnp.zeros((half_cells, width), F32)
            for h, m in enumerate(in_head):
                total = jnp.where(m, mixed[h * half_cells:(h + 1) * half_cells], total)
            attended.append(total)
            if s % 2 == 1:
                @pl.when(t == 0)
                def _():
                    hand_on(2 + s // 2)
        att_n[:, :width] = jnp.concatenate(attended, axis=0).astype(BF16)
        weights_here(t, 1)
        middle = (grid + mm_nt(att_n[...], proj[...])).astype(BF16).astype(F32)
        pick_row = (lax.broadcasted_iota(jnp.int32, (16, wide), 1) == width + 1).astype(F32).astype(BF16)
        shift_out = mm_nt(pick_row, proj[...])[:1]
        own_n[:, :width] = layer_norm(middle, g2, s2).astype(BF16)
        weights_here(t, 2)
        weights_here(t, 3)
        for part in range(chunks):
            cut = slice(part * chunk, (part + 1) * chunk)
            result = middle[cut] + shift_out
            for i in range(tp):
                pre = mm(own_n[cut, :], expand[i])
                hidden = (0.5 * pre * (1.0 + lax.erf(pre * float(np.sqrt(0.5))))).astype(BF16)
                result = result + mm(hidden, reduce[i])
            outp[t, cut, :] = result.astype(BF16)

            @pl.when(section == 0)
            def _():
                state_copy(t, 0, part).start()
                if part == chunks - 1:
                    state_copy(t, 1, part).start()

        out_ref[t] = mm(unperm[...], outp[t]).astype(BF16)
        return carry

    lax.fori_loop(0, micro, turn, 0)

    for kind in range(4):
        for way in range(3):
            weight_copy(kind, way).wait_send()

    @pl.when(section == 0)
    def _():
        field_copy().wait_send()
        for t in range(micro):
            for part in range(chunks):
                state_copy(t, 0, part).wait_send()
            state_copy(t, 1, chunks - 1).wait_send()

    @pl.when(section == 1)
    def _():
        for t in range(micro):
            for part in range(chunks - 1):
                state_forward(t, part).wait_send()


def on_device(
    initial_field, first_gain, first_shift, qkv_weight, qkv_bias, proj_weight, proj_bias,
    second_gain, second_shift, expand_weight, expand_bias, reduce_weight, reduce_bias, earth_bias,
):
    tp = lax.axis_size("tp")
    micro, levels, lat_rows, lon, width = initial_field.shape
    cells = levels * lat_rows * lon
    heads, entries = earth_bias.shape[-2:]
    slabs = lon // WW
    half_cells = cells // slabs
    wide = -(-(width + 2) // 128) * 128
    lines = -(-heads * GROUP // 8) * 8
    chunks = 2
    lanes = -(-WZ * WH * (2 * WW - 1) // 128) * 128
    q_weight, p_weight = qkv_weight[0].T, proj_weight[0].T
    vmem = pl.BlockSpec(memory_space=pltpu.VMEM)
    dma = pltpu.SemaphoreType.DMA
    out = pl.pallas_call(
        functools.partial(kernel, tp, micro, heads, slabs),
        out_shape=jax.ShapeDtypeStruct((micro, cells, width), BF16),
        in_specs=[pl.BlockSpec(memory_space=pltpu.HBM)] * 14,
        out_specs=vmem,
        scratch_shapes=[
            pltpu.VMEM((micro, cells, width), BF16),
            pltpu.VMEM((1, width), BF16),
            pltpu.VMEM((1, width), BF16),
            pltpu.VMEM(q_weight.shape, BF16),
            pltpu.VMEM(qkv_bias.shape, BF16),
            pltpu.VMEM(p_weight.shape, BF16),
            pltpu.VMEM(proj_bias.shape, BF16),
            pltpu.VMEM((1, width), BF16),
            pltpu.VMEM((1, width), BF16),
            pltpu.VMEM((width, width), BF16),
            pltpu.VMEM((1, width), BF16),
            pltpu.VMEM(reduce_bias.shape, BF16),
            pltpu.VMEM((heads, 1, entries), F32),
            pltpu.VMEM((3 * width, wide), BF16),
            pltpu.VMEM((width, wide), BF16),
            pltpu.VMEM((tp, wide, width), BF16),
            pltpu.VMEM((tp, width, width), BF16),
            pltpu.VMEM((micro, cells, width), BF16),
            pltpu.VMEM((micro, 2, cells, width), BF16),
            pltpu.VMEM((micro, cells, width), BF16),
            pltpu.VMEM((cells, cells), BF16),
            pltpu.VMEM((cells, cells), BF16),
            pltpu.VMEM((cells, wide), BF16),
            pltpu.VMEM((cells, wide), BF16),
            pltpu.VMEM((cells, wide), BF16),
            pltpu.VMEM((lines, lanes), F32),
            pltpu.VMEM((heads * half_cells, 2 * half_cells), F32),
            dma((14,)),
            dma((4, 3)),
            dma((4, 3)),
            dma,
            dma,
            dma((micro, 2, chunks)),
            dma((micro, 2, chunks)),
        ],
        compiler_params=pltpu.CompilerParams(
            collective_id=0, has_side_effects=True, vmem_limit_bytes=60 * 1024 * 1024),
    )(
        initial_field.reshape(micro, cells, width), first_gain, first_shift, q_weight, qkv_bias,
        p_weight, proj_bias, second_gain, second_shift, expand_weight[0], expand_bias,
        reduce_weight[0], reduce_bias, earth_bias.reshape(heads, 1, entries),
    )
    return out.reshape(1, micro, levels, lat_rows, lon, width)


def solution(mesh):
    return jax.shard_map(
        on_device,
        mesh=mesh,
        in_specs=(
            P(None, "tp", "lat", None, None),
            P("section", None),
            P("section", None),
            P("section", None, "tp"),
            P("section", "tp"),
            P("section", None, "tp"),
            P("section", "tp"),
            P("section", None),
            P("section", None),
            P("section", None, "tp"),
            P("section", "tp"),
            P("section", "tp", None),
            P("section", "tp"),
            P("section", "tp", "lat", None, None),
        ),
        out_specs=P("section", None, "tp", "lat", None, None),
        check_vma=False,
    )
```

```python
import functools

import jax
import jax.numpy as jnp
import numpy as np
from jax import lax
from jax.experimental import pallas as pl
from jax.experimental.pallas import tpu as pltpu
from jax.sharding import PartitionSpec as P

WZ = 2
WH = 6
WW = 12
HALF = WH // 2
GROUP = WZ * HALF
EPS = 1e-05
MESH = pl.DeviceIdType.MESH
F32 = jnp.float32
BF16 = jnp.bfloat16
NT = (((1,), (1,)), ((), ()))
TN = (((0,), (0,)), ((), ()))
LOG2E = float(np.log2(np.e))


def mm(a, b):
    return jnp.dot(a, b, preferred_element_type=F32)


def mm_nt(a, b):
    return lax.dot_general(a, b, NT, preferred_element_type=F32)


def layer_norm(values, gain, shift):
    mean = jnp.mean(values, axis=-1, keepdims=True)
    centred = values - mean
    spread = jnp.mean(centred * centred, axis=-1, keepdims=True)
    return centred * lax.rsqrt(spread + EPS) * gain + shift


def kernel(
    tp, micro, heads, slabs, edges,
    x_in, g1_in, s1_in, qw_in, qb_in, pw_in, pb_in, g2_in, s2_in,
    ew_in, eb_in, rw_in, rb_in, table_in,
    out_ref,
    x_ref, g1_ref, s1_ref, qw_ref, qb_ref, pw_ref, pb_ref, g2_ref, s2_ref,
    ew_ref, eb_ref, rb_ref, table_ref,
    qkv, proj, expand, reduce, near, inbuf, outp, perm, unperm,
    own_n, near_n, att_n, table, spread, bias,
    l_sem, w_send, w_recv, f_send, f_recv, o_send, o_recv,
):
    me = lax.axis_index("tp")
    lat = lax.axis_index("lat")
    section = lax.axis_index("section")
    pair = lat + 1 - 2 * lax.rem(lat, 2)
    other = 1 - section
    cells, width = x_ref.shape[1:]
    wide = own_n.shape[1]
    half_cells = cells // slabs
    head_size = width // heads
    q_part, p_part, e_part = qw_ref.shape[0], pw_ref.shape[0], ew_ref.shape[1]
    core_peer = me + 1 - 2 * lax.rem(me, 2)
    chip_peer = lax.rem(me + tp // 2, tp)

    barrier = pltpu.get_barrier_semaphore()
    pl.semaphore_signal(barrier, inc=1, device_id={"tp": core_peer}, device_id_type=MESH)
    pl.semaphore_signal(barrier, inc=1, device_id={"tp": chip_peer}, device_id_type=MESH)
    pl.semaphore_signal(barrier, inc=1, device_id={"lat": pair}, device_id_type=MESH)
    pl.semaphore_signal(barrier, inc=1, device_id={"section": other}, device_id_type=MESH)
    pl.semaphore_signal(barrier, inc=1, device_id={"section": other, "lat": pair}, device_id_type=MESH)

    loads = [
        pltpu.make_async_copy(source, target, l_sem.at[n])
        for n, (source, target) in enumerate((
            (qw_in, qw_ref), (qb_in, qb_ref), (pw_in, pw_ref), (pb_in, pb_ref), (rb_in, rb_ref),
            (ew_in, ew_ref), (eb_in, eb_ref), (rw_in, reduce.at[pl.ds(pl.multiple_of(me * e_part, 16), e_part), :]), (x_in, x_ref), (table_in, table_ref),
            (g1_in, g1_ref), (s1_in, s1_ref), (g2_in, g2_ref), (s2_in, s2_ref),
        ))
    ]
    for load in loads:
        load.start()


    def owner_rows(owner, part):
        return pl.ds(pl.multiple_of(owner * part, 16), part)

    for load in loads[:5]:
        load.wait()
    tail = lax.broadcasted_iota(jnp.int32, (wide - width, q_part), 0)
    q_tail = jnp.where(tail == 0, qb_ref[...].astype(F32), 0.0).T
    qkv[owner_rows(me, q_part), :] = jnp.concatenate(
        [qw_ref[...].astype(F32), q_tail], axis=1).astype(BF16)
    tail = lax.broadcasted_iota(jnp.int32, (wide - width, p_part), 0)
    p_tail = jnp.where(
        tail == 0, pb_ref[...].astype(F32), jnp.where(tail == 1, rb_ref[...].astype(F32), 0.0)).T
    proj[owner_rows(me, p_part), :] = jnp.concatenate(
        [pw_ref[...].astype(F32), p_tail], axis=1).astype(BF16)
    for load in loads[5:8]:
        load.wait()
    tail = lax.broadcasted_iota(jnp.int32, (wide - width, e_part), 0)
    expand[owner_rows(me, e_part), :] = jnp.concatenate(
        [ew_ref[...].astype(F32), jnp.where(tail == 0, eb_ref[...].astype(F32), 0.0)], axis=0).T.astype(BF16)

    pl.semaphore_wait(barrier, 5)

    def weight_copy(kind, way):
        owner = chip_peer if way == 2 else me
        ref = (
            lambda: qkv.at[owner_rows(owner, q_part), :],
            lambda: proj.at[owner_rows(owner, p_part), :],
            lambda: expand.at[owner_rows(owner, e_part), :],
            lambda: reduce.at[owner_rows(owner, e_part), :],
        )[kind]()
        return pltpu.make_async_remote_copy(
            src_ref=ref, dst_ref=ref, send_sem=w_send.at[kind, way], recv_sem=w_recv.at[kind, way],
            device_id={"tp": chip_peer if way == 1 else core_peer}, device_id_type=MESH)

    def hand_on(kind):
        weight_copy(kind, 1).wait_recv()
        weight_copy(kind, 2).start()

    def field_copy():
        return pltpu.make_async_remote_copy(
            src_ref=x_in, dst_ref=near, send_sem=f_send, recv_sem=f_recv,
            device_id={"lat": pair}, device_id_type=MESH)

    chunks = len(edges) - 1

    def state_copy(t, which, part):
        rows = pl.ds(edges[part], edges[part + 1] - edges[part])
        target = {"section": other} if which == 0 else {"section": other, "lat": pair}
        return pltpu.make_async_remote_copy(
            src_ref=outp.at[t, rows], dst_ref=inbuf.at[t, which, rows], send_sem=o_send.at[t, which, part],
            recv_sem=o_recv.at[t, which, part], device_id=target, device_id_type=MESH)

    def state_forward(t, part):
        rows = pl.ds(edges[part], edges[part + 1] - edges[part])
        return pltpu.make_async_remote_copy(
            src_ref=inbuf.at[t, 0, rows], dst_ref=inbuf.at[t, 1, rows], send_sem=o_send.at[t, 1, part],
            recv_sem=o_recv.at[t, 1, part], device_id={"lat": pair}, device_id_type=MESH)

    for way in (0, 1):
        weight_copy(0, way).start()

    @pl.when(section == 0)
    def _():
        field_copy().start()

    for kind in (1, 2, 3):
        for way in (0, 1):
            weight_copy(kind, way).start()
    for load in loads[8:]:
        load.wait()

    stretch = cells // GROUP
    step = -(-65536 // GROUP)
    line = lax.broadcasted_iota(jnp.int32, (1, cells), 1)
    level_row = sum((line >= stretch * k).astype(jnp.int32) for k in range(1, GROUP))
    forth = (line - stretch * level_row) * GROUP + level_row
    column = lax.shift_right_logical(line * step, 16)
    back = (line - GROUP * column) * stretch + column
    rows = lax.broadcasted_iota(jnp.int32, (cells, cells), 0)
    perm[...] = (rows == forth).astype(F32).astype(BF16)
    unperm[...] = (rows == back).astype(F32).astype(BF16)
    lanes = lax.broadcasted_iota(jnp.int32, (cells, wide), 1)
    ones = (lanes == width).astype(F32).astype(BF16)
    own_n[...] = ones
    near_n[...] = ones
    att_n[...] = ones

    @pl.when(section == 0)
    def _():
        for t in range(micro):
            inbuf[t, 0] = mm(perm[...], x_ref[t]).astype(BF16)

    hand_on(0)

    table[...] = jnp.zeros_like(table)
    span = WH * (2 * WW - 1)
    for zq in range(WZ):
        for zk in range(WZ):
            for r in range(HALF):
                off = ((zq * WZ + zk) * HALF + r) * span
                piece = table_ref[:, 0, off:off + span]
                for h in range(heads):
                    row = h * GROUP + zq * HALF + r
                    table[row:row + 1, zk * span:(zk + 1) * span] = piece[h:h + 1]
    c = lax.broadcasted_iota(jnp.int32, (1, 2 * half_cells), 1)
    far = (c >= half_cells).astype(jnp.int32)
    c = c - half_cells * far
    wk = sum((c >= GROUP * k).astype(jnp.int32) for k in range(1, WW))
    zr = c - GROUP * wk
    zk = (zr >= HALF).astype(jnp.int32)
    band = lax.rem(lat, 2)
    hk = zr - HALF * zk + HALF * (band + far - 2 * band * far)
    place = zk * span + hk * (2 * WW - 1) + WW - 1 - wk
    pick = (lax.broadcasted_iota(jnp.int32, (table.shape[1], 2 * half_cells), 0) == place).astype(F32).astype(BF16)
    full = table[...]
    lines = full.shape[0]
    for wq in range(WW):
        turned = full if wq == 0 else pltpu.roll(full, full.shape[1] - wq, 1)
        first = turned.astype(BF16)
        rest = turned - first.astype(F32)
        second = rest.astype(BF16)
        third = (rest - second.astype(F32)).astype(BF16)
        parts = mm(
            jnp.concatenate([p.astype(F32) for p in (first, second, third)], axis=0).astype(BF16), pick)
        total = parts[:lines] + parts[lines:2 * lines] + parts[2 * lines:]
        for h in range(heads):
            at = h * half_cells + wq * GROUP
            spread[at:at + GROUP, :] = total[h * GROUP:(h + 1) * GROUP]
    bias[...] = spread[...].T * LOG2E

    hand_on(1)

    @pl.when(section == 0)
    def _():
        field_copy().wait_recv()
        for t in range(micro):
            inbuf[t, 1] = mm(perm[...], near[t]).astype(BF16)

    scale = LOG2E / float(np.sqrt(head_size))
    lane_head = lax.broadcasted_iota(jnp.int32, (half_cells, width), 1)
    in_head = [(lane_head >= h * head_size) & (lane_head < (h + 1) * head_size) for h in range(heads)]

    def weights_here(t, kind):
        @pl.when(t == 0)
        def _():
            weight_copy(kind, 0).wait_recv()
            weight_copy(kind, 2).wait_recv()

    def turn(t, carry):
        @pl.when(section == 1)
        def _():
            for part in range(chunks):
                state_copy(t, 0, part).wait_recv()
                if part < chunks - 1:
                    state_forward(t, part).start()

        g1, s1 = g1_ref[...].astype(F32), s1_ref[...].astype(F32)
        g2, s2 = g2_ref[...].astype(F32), s2_ref[...].astype(F32)
        grid = inbuf[t, 0].astype(F32)
        own_n[:, :width] = layer_norm(grid, g1, s1).astype(BF16)
        weights_here(t, 0)
        q = mm_nt(own_n[...], qkv[:width, :])
        k_own = mm_nt(own_n[...], qkv[width:2 * width, :])
        v_own = mm_nt(own_n[...], qkv[2 * width:, :])

        @pl.when(section == 1)
        def _():
            for part in range(chunks):
                state_copy(t, 1, part).wait_recv()

        near_n[:, :width] = layer_norm(inbuf[t, 1].astype(F32), g1, s1).astype(BF16)
        k_near = mm_nt(near_n[...], qkv[width:2 * width, :])
        v_near = mm_nt(near_n[...], qkv[2 * width:, :])
        attended = []
        for s in range(slabs):
            cut = slice(s * half_cells, (s + 1) * half_cells)
            keys = jnp.concatenate([k_own[cut], k_near[cut]], axis=0).astype(BF16)
            vals = jnp.concatenate([v_own[cut], v_near[cut]], axis=0).astype(BF16)
            stack = jnp.concatenate([jnp.where(m, q[cut], 0.0) for m in in_head], axis=0).astype(BF16)
            scores = mm_nt(keys, stack) * scale + bias[...]
            e = jnp.exp2(scores - jnp.max(scores, axis=0, keepdims=True))
            probs = (e * (1.0 / jnp.sum(e, axis=0, keepdims=True))).astype(BF16)
            mixed = lax.dot_general(probs, vals, TN, preferred_element_type=F32)
            total = jnp.zeros((half_cells, width), F32)
            for h, m in enumerate(in_head):
                total = jnp.where(m, mixed[h * half_cells:(h + 1) * half_cells], total)
            attended.append(total)
            if s in (0, 2):
                @pl.when(t == 0)
                def _():
                    hand_on(2 + s // 2)
        att_n[:, :width] = jnp.concatenate(attended, axis=0).astype(BF16)
        weights_here(t, 1)
        middle = (grid + mm_nt(att_n[...], proj[...])).astype(BF16).astype(F32)
        pick_row = (lax.broadcasted_iota(jnp.int32, (16, wide), 1) == width + 1).astype(F32).astype(BF16)
        shift_out = mm_nt(pick_row, proj[...])[:1]
        own_n[:, :width] = layer_norm(middle, g2, s2).astype(BF16)
        weights_here(t, 2)
        for part in range(chunks):
            cut = slice(edges[part], edges[part + 1])
            pre = mm_nt(own_n[cut, :], expand[...])
            hidden = (0.5 * pre * (1.0 + lax.erf(pre * float(np.sqrt(0.5))))).astype(BF16)
            if part == 0:
                weights_here(t, 3)
            result = middle[cut] + shift_out + mm(hidden, reduce[...])
            outp[t, cut, :] = result.astype(BF16)

            @pl.when(section == 0)
            def _():
                state_copy(t, 0, part).start()
                if part == chunks - 1:
                    state_copy(t, 1, part).start()

        out_ref[t] = mm(unperm[...], outp[t]).astype(BF16)
        return carry

    lax.fori_loop(0, micro, turn, 0)

    for kind in range(4):
        for way in range(3):
            weight_copy(kind, way).wait_send()

    @pl.when(section == 0)
    def _():
        field_copy().wait_send()
        for t in range(micro):
            for part in range(chunks):
                state_copy(t, 0, part).wait_send()
            state_copy(t, 1, chunks - 1).wait_send()

    @pl.when(section == 1)
    def _():
        for t in range(micro):
            for part in range(chunks - 1):
                state_forward(t, part).wait_send()


def on_device(
    initial_field, first_gain, first_shift, qkv_weight, qkv_bias, proj_weight, proj_bias,
    second_gain, second_shift, expand_weight, expand_bias, reduce_weight, reduce_bias, earth_bias,
):
    tp = lax.axis_size("tp")
    micro, levels, lat_rows, lon, width = initial_field.shape
    cells = levels * lat_rows * lon
    heads, entries = earth_bias.shape[-2:]
    slabs = lon // WW
    half_cells = cells // slabs
    hidden = expand_weight.shape[2]
    wide = -(-(width + 2) // 128) * 128
    lines = -(-heads * GROUP // 8) * 8
    tiles = cells // 16
    edges = (0, tiles // 2 * 16, (tiles - tiles // 6) * 16, cells)
    chunks = len(edges) - 1
    lanes = -(-WZ * WH * (2 * WW - 1) // 128) * 128
    q_weight, p_weight = qkv_weight[0].T, proj_weight[0].T
    vmem = pl.BlockSpec(memory_space=pltpu.VMEM)
    dma = pltpu.SemaphoreType.DMA
    out = pl.pallas_call(
        functools.partial(kernel, tp, micro, heads, slabs, edges),
        out_shape=jax.ShapeDtypeStruct((micro, cells, width), BF16),
        in_specs=[pl.BlockSpec(memory_space=pltpu.HBM)] * 14,
        out_specs=vmem,
        scratch_shapes=[
            pltpu.VMEM((micro, cells, width), BF16),
            pltpu.VMEM((1, width), BF16),
            pltpu.VMEM((1, width), BF16),
            pltpu.VMEM(q_weight.shape, BF16),
            pltpu.VMEM(qkv_bias.shape, BF16),
            pltpu.VMEM(p_weight.shape, BF16),
            pltpu.VMEM(proj_bias.shape, BF16),
            pltpu.VMEM((1, width), BF16),
            pltpu.VMEM((1, width), BF16),
            pltpu.VMEM((width, hidden), BF16),
            pltpu.VMEM((1, hidden), BF16),
            pltpu.VMEM(reduce_bias.shape, BF16),
            pltpu.VMEM((heads, 1, entries), F32),
            pltpu.VMEM((3 * width, wide), BF16),
            pltpu.VMEM((width, wide), BF16),
            pltpu.VMEM((tp * hidden, wide), BF16),
            pltpu.VMEM((tp * hidden, width), BF16),
            pltpu.VMEM((micro, cells, width), BF16),
            pltpu.VMEM((micro, 2, cells, width), BF16),
            pltpu.VMEM((micro, cells, width), BF16),
            pltpu.VMEM((cells, cells), BF16),
            pltpu.VMEM((cells, cells), BF16),
            pltpu.VMEM((cells, wide), BF16),
            pltpu.VMEM((cells, wide), BF16),
            pltpu.VMEM((cells, wide), BF16),
            pltpu.VMEM((lines, lanes), F32),
            pltpu.VMEM((heads * half_cells, 2 * half_cells), F32),
            pltpu.VMEM((2 * half_cells, heads * half_cells), F32),
            dma((14,)),
            dma((4, 3)),
            dma((4, 3)),
            dma,
            dma,
            dma((micro, 2, chunks)),
            dma((micro, 2, chunks)),
        ],
        compiler_params=pltpu.CompilerParams(
            collective_id=0, has_side_effects=True, vmem_limit_bytes=60 * 1024 * 1024),
    )(
        initial_field.reshape(micro, cells, width), first_gain, first_shift, q_weight, qkv_bias,
        p_weight, proj_bias, second_gain, second_shift, expand_weight[0], expand_bias,
        reduce_weight[0], reduce_bias, earth_bias.reshape(heads, 1, entries),
    )
    return out.reshape(1, micro, levels, lat_rows, lon, width)


def solution(mesh):
    return jax.shard_map(
        on_device,
        mesh=mesh,
        in_specs=(
            P(None, "tp", "lat", None, None),
            P("section", None),
            P("section", None),
            P("section", None, "tp"),
            P("section", "tp"),
            P("section", None, "tp"),
            P("section", "tp"),
            P("section", None),
            P("section", None),
            P("section", None, "tp"),
            P("section", "tp"),
            P("section", "tp", None),
            P("section", "tp"),
            P("section", "tp", "lat", None, None),
        ),
        out_specs=P("section", None, "tp", "lat", None, None),
        check_vma=False,
    )
```

```python
import functools

import jax
import jax.numpy as jnp
import numpy as np
from jax import lax
from jax.experimental import pallas as pl
from jax.experimental.pallas import tpu as pltpu
from jax.sharding import PartitionSpec as P

WZ = 2
WH = 6
WW = 12
HALF = WH // 2
GROUP = WZ * HALF
EPS = 1e-05
MESH = pl.DeviceIdType.MESH
F32 = jnp.float32
BF16 = jnp.bfloat16
NT = (((1,), (1,)), ((), ()))
TN = (((0,), (0,)), ((), ()))
LOG2E = float(np.log2(np.e))


def mm(a, b):
    return jnp.dot(a, b, preferred_element_type=F32)


def mm_nt(a, b):
    return lax.dot_general(a, b, NT, preferred_element_type=F32)


def layer_norm(values, gain, shift):
    mean = jnp.mean(values, axis=-1, keepdims=True)
    centred = values - mean
    spread = jnp.mean(centred * centred, axis=-1, keepdims=True)
    return centred * lax.rsqrt(spread + EPS) * gain + shift


def kernel(
    tp, micro, heads, slabs, edges,
    x_in, g1_in, s1_in, qw_in, qb_in, pw_in, pb_in, g2_in, s2_in,
    ew_in, eb_in, rw_in, rb_in, table_in,
    out_ref,
    x_ref, g1_ref, s1_ref, qw_ref, qb_ref, pw_ref, pb_ref, g2_ref, s2_ref,
    ew_ref, eb_ref, rb_ref, table_ref,
    qkv, proj, expand, reduce, near, inbuf, outp, perm, unperm,
    own_n, near_n, att_n, table, spread, bias,
    l_sem, w_send, w_recv, f_send, f_recv, o_send, o_recv,
):
    me = lax.axis_index("tp")
    lat = lax.axis_index("lat")
    section = lax.axis_index("section")
    pair = lat + 1 - 2 * lax.rem(lat, 2)
    other = 1 - section
    cells, width = x_ref.shape[1:]
    wide = own_n.shape[1]
    half_cells = cells // slabs
    head_size = width // heads
    q_part, p_part, e_part = qw_ref.shape[0], pw_ref.shape[0], ew_ref.shape[1]
    core_peer = me + 1 - 2 * lax.rem(me, 2)
    chip_peer = lax.rem(me + tp // 2, tp)

    barrier = pltpu.get_barrier_semaphore()
    pl.semaphore_signal(barrier, inc=1, device_id={"tp": core_peer}, device_id_type=MESH)
    pl.semaphore_signal(barrier, inc=1, device_id={"tp": chip_peer}, device_id_type=MESH)
    pl.semaphore_signal(barrier, inc=1, device_id={"lat": pair}, device_id_type=MESH)
    pl.semaphore_signal(barrier, inc=1, device_id={"section": other}, device_id_type=MESH)
    pl.semaphore_signal(barrier, inc=1, device_id={"section": other, "lat": pair}, device_id_type=MESH)

    loads = [
        pltpu.make_async_copy(source, target, l_sem.at[n])
        for n, (source, target) in enumerate((
            (qw_in, qw_ref), (qb_in, qb_ref), (pw_in, pw_ref), (pb_in, pb_ref), (rb_in, rb_ref),
            (ew_in, ew_ref), (eb_in, eb_ref), (rw_in, reduce.at[pl.ds(pl.multiple_of(me * e_part, 16), e_part), :]), (x_in, x_ref), (table_in, table_ref),
            (g1_in, g1_ref), (s1_in, s1_ref), (g2_in, g2_ref), (s2_in, s2_ref),
        ))
    ]
    for load in loads:
        load.start()


    def owner_rows(owner, part):
        return pl.ds(pl.multiple_of(owner * part, 16), part)

    for load in loads[:5]:
        load.wait()
    tail = lax.broadcasted_iota(jnp.int32, (wide - width, q_part), 0)
    q_tail = jnp.where(tail == 0, qb_ref[...].astype(F32), 0.0).T
    qkv[owner_rows(me, q_part), :] = jnp.concatenate(
        [qw_ref[...].astype(F32), q_tail], axis=1).astype(BF16)
    tail = lax.broadcasted_iota(jnp.int32, (wide - width, p_part), 0)
    p_tail = jnp.where(
        tail == 0, pb_ref[...].astype(F32), jnp.where(tail == 1, rb_ref[...].astype(F32), 0.0)).T
    proj[owner_rows(me, p_part), :] = jnp.concatenate(
        [pw_ref[...].astype(F32), p_tail], axis=1).astype(BF16)
    for load in loads[5:8]:
        load.wait()
    tail = lax.broadcasted_iota(jnp.int32, (wide - width, e_part), 0)
    expand[owner_rows(me, e_part), :] = jnp.concatenate(
        [ew_ref[...].astype(F32), jnp.where(tail == 0, eb_ref[...].astype(F32), 0.0)], axis=0).T.astype(BF16)

    pl.semaphore_wait(barrier, 5)

    def weight_copy(kind, way):
        owner = chip_peer if way == 2 else me
        ref = (
            lambda: qkv.at[owner_rows(owner, q_part), :],
            lambda: proj.at[owner_rows(owner, p_part), :],
            lambda: expand.at[owner_rows(owner, e_part), :],
            lambda: reduce.at[owner_rows(owner, e_part), :],
        )[kind]()
        return pltpu.make_async_remote_copy(
            src_ref=ref, dst_ref=ref, send_sem=w_send.at[kind, way], recv_sem=w_recv.at[kind, way],
            device_id={"tp": chip_peer if way == 1 else core_peer}, device_id_type=MESH)

    def hand_on(kind):
        weight_copy(kind, 1).wait_recv()
        weight_copy(kind, 2).start()

    def field_copy():
        return pltpu.make_async_remote_copy(
            src_ref=x_in, dst_ref=near, send_sem=f_send, recv_sem=f_recv,
            device_id={"lat": pair}, device_id_type=MESH)

    chunks = len(edges) - 1

    def state_copy(t, which, part):
        rows = pl.ds(edges[part], edges[part + 1] - edges[part])
        target = {"section": other} if which == 0 else {"section": other, "lat": pair}
        return pltpu.make_async_remote_copy(
            src_ref=outp.at[t, rows], dst_ref=inbuf.at[t, which, rows], send_sem=o_send.at[t, which, part],
            recv_sem=o_recv.at[t, which, part], device_id=target, device_id_type=MESH)

    def state_forward(t, part):
        rows = pl.ds(edges[part], edges[part + 1] - edges[part])
        return pltpu.make_async_remote_copy(
            src_ref=inbuf.at[t, 0, rows], dst_ref=inbuf.at[t, 1, rows], send_sem=o_send.at[t, 1, part],
            recv_sem=o_recv.at[t, 1, part], device_id={"lat": pair}, device_id_type=MESH)

    for way in (0, 1):
        weight_copy(0, way).start()

    @pl.when(section == 0)
    def _():
        field_copy().start()

    for kind in (1, 2, 3):
        for way in (0, 1):
            weight_copy(kind, way).start()
    for load in loads[8:]:
        load.wait()

    stretch = cells // GROUP
    step = -(-65536 // GROUP)
    line = lax.broadcasted_iota(jnp.int32, (1, cells), 1)
    level_row = sum((line >= stretch * k).astype(jnp.int32) for k in range(1, GROUP))
    forth = (line - stretch * level_row) * GROUP + level_row
    column = lax.shift_right_logical(line * step, 16)
    back = (line - GROUP * column) * stretch + column
    rows = lax.broadcasted_iota(jnp.int32, (cells, cells), 0)
    perm[...] = (rows == forth).astype(F32).astype(BF16)
    unperm[...] = (rows == back).astype(F32).astype(BF16)
    lanes = lax.broadcasted_iota(jnp.int32, (cells, wide), 1)
    ones = (lanes == width).astype(F32).astype(BF16)
    own_n[...] = ones
    near_n[...] = ones
    att_n[...] = ones

    table[...] = jnp.zeros_like(table)
    span = WH * (2 * WW - 1)
    for zq in range(WZ):
        for zk in range(WZ):
            for r in range(HALF):
                off = ((zq * WZ + zk) * HALF + r) * span
                piece = table_ref[:, 0, off:off + span]
                for h in range(heads):
                    row = h * GROUP + zq * HALF + r
                    table[row:row + 1, zk * span:(zk + 1) * span] = piece[h:h + 1]
    c = lax.broadcasted_iota(jnp.int32, (1, 2 * half_cells), 1)
    far = (c >= half_cells).astype(jnp.int32)
    c = c - half_cells * far
    wk = sum((c >= GROUP * k).astype(jnp.int32) for k in range(1, WW))
    zr = c - GROUP * wk
    zk = (zr >= HALF).astype(jnp.int32)
    band = lax.rem(lat, 2)
    hk = zr - HALF * zk + HALF * (band + far - 2 * band * far)
    place = zk * span + hk * (2 * WW - 1) + WW - 1 - wk
    pick = (lax.broadcasted_iota(jnp.int32, (table.shape[1], 2 * half_cells), 0) == place).astype(F32).astype(BF16)
    full = table[...]
    lines = full.shape[0]
    turned = jnp.concatenate(
        [full if wq == 0 else pltpu.roll(full, full.shape[1] - wq, 1) for wq in range(WW)], axis=0)
    first = turned.astype(BF16)
    rest = turned - first.astype(F32)
    second = rest.astype(BF16)
    third = (rest - second.astype(F32)).astype(BF16)
    hand_on(0)
    total = mm(first, pick) + mm(second, pick) + mm(third, pick)
    for wq in range(WW):
        for h in range(heads):
            at, row = h * half_cells + wq * GROUP, wq * lines + h * GROUP
            spread[at:at + GROUP, :] = total[row:row + GROUP]
    bias[...] = spread[...].T * LOG2E

    hand_on(1)

    @pl.when(section == 0)
    def _():
        field_copy().wait_recv()

    scale = LOG2E / float(np.sqrt(head_size))
    lane_head = lax.broadcasted_iota(jnp.int32, (half_cells, width), 1)
    in_head = [(lane_head >= h * head_size) & (lane_head < (h + 1) * head_size) for h in range(heads)]

    def weights_here(t, kind):
        @pl.when(t == 0)
        def _():
            weight_copy(kind, 0).wait_recv()
            weight_copy(kind, 2).wait_recv()

    def turn(t, carry):
        @pl.when(section == 0)
        def _():
            inbuf[t, 0] = mm(perm[...], x_ref[t]).astype(BF16)
            inbuf[t, 1] = mm(perm[...], near[t]).astype(BF16)

        @pl.when(section == 1)
        def _():
            for part in range(chunks):
                state_copy(t, 0, part).wait_recv()
                if part < chunks - 1:
                    @pl.when(t == 0)
                    def _():
                        state_forward(t, part).start()

        g1, s1 = g1_ref[...].astype(F32), s1_ref[...].astype(F32)
        g2, s2 = g2_ref[...].astype(F32), s2_ref[...].astype(F32)
        grid = inbuf[t, 0].astype(F32)
        own_n[:, :width] = layer_norm(grid, g1, s1).astype(BF16)
        weights_here(t, 0)
        q = mm_nt(own_n[...], qkv[:width, :])
        k_own = mm_nt(own_n[...], qkv[width:2 * width, :])
        v_own = mm_nt(own_n[...], qkv[2 * width:, :])

        @pl.when(section == 1)
        def _():
            for part in range(chunks):
                state_copy(t, 1, part).wait_recv()

        near_n[:, :width] = layer_norm(inbuf[t, 1].astype(F32), g1, s1).astype(BF16)
        k_near = mm_nt(near_n[...], qkv[width:2 * width, :])
        v_near = mm_nt(near_n[...], qkv[2 * width:, :])

        @pl.when(t == 0)
        def _():
            hand_on(2)

        attended = []
        for s in range(slabs):
            cut = slice(s * half_cells, (s + 1) * half_cells)
            keys = jnp.concatenate([k_own[cut], k_near[cut]], axis=0).astype(BF16)
            vals = jnp.concatenate([v_own[cut], v_near[cut]], axis=0).astype(BF16)
            stack = jnp.concatenate([jnp.where(m, q[cut], 0.0) for m in in_head], axis=0).astype(BF16)
            scores = mm_nt(keys, stack) * scale + bias[...]
            e = jnp.exp2(scores - jnp.max(scores, axis=0, keepdims=True))
            probs = (e * (1.0 / jnp.sum(e, axis=0, keepdims=True))).astype(BF16)
            mixed = lax.dot_general(probs, vals, TN, preferred_element_type=F32)
            total = jnp.zeros((half_cells, width), F32)
            for h, m in enumerate(in_head):
                total = jnp.where(m, mixed[h * half_cells:(h + 1) * half_cells], total)
            attended.append(total)
        att_n[:, :width] = jnp.concatenate(attended, axis=0).astype(BF16)

        @pl.when(t == 0)
        def _():
            hand_on(3)

        weights_here(t, 1)
        middle = (grid + mm_nt(att_n[...], proj[...])).astype(BF16).astype(F32)
        pick_row = (lax.broadcasted_iota(jnp.int32, (16, wide), 1) == width + 1).astype(F32).astype(BF16)
        shift_out = mm_nt(pick_row, proj[...])[:1]
        own_n[:, :width] = layer_norm(middle, g2, s2).astype(BF16)
        weights_here(t, 2)
        for part in range(chunks):
            cut = slice(edges[part], edges[part + 1])
            pre = mm_nt(own_n[cut, :], expand[...])
            hidden = (0.5 * pre * (1.0 + lax.erf(pre * float(np.sqrt(0.5))))).astype(BF16)
            if part == 0:
                weights_here(t, 3)
            result = middle[cut] + shift_out + mm(hidden, reduce[...])
            outp[t, cut, :] = result.astype(BF16)

            @pl.when(section == 0)
            def _():
                state_copy(t, 0, part).start()
                if part == chunks - 1:
                    @pl.when(t > 0)
                    def _():
                        for early in range(chunks - 1):
                            state_copy(t, 1, early).start()
                    state_copy(t, 1, part).start()

        out_ref[t] = mm(unperm[...], outp[t]).astype(BF16)
        return carry

    lax.fori_loop(0, micro, turn, 0)

    for kind in range(4):
        for way in range(3):
            weight_copy(kind, way).wait_send()

    @pl.when(section == 0)
    def _():
        field_copy().wait_send()
        for t in range(micro):
            for part in range(chunks):
                state_copy(t, 0, part).wait_send()
                if t > 0 or part == chunks - 1:
                    state_copy(t, 1, part).wait_send()

    @pl.when(section == 1)
    def _():
        for part in range(chunks - 1):
            state_forward(0, part).wait_send()


def on_device(
    initial_field, first_gain, first_shift, qkv_weight, qkv_bias, proj_weight, proj_bias,
    second_gain, second_shift, expand_weight, expand_bias, reduce_weight, reduce_bias, earth_bias,
):
    tp = lax.axis_size("tp")
    micro, levels, lat_rows, lon, width = initial_field.shape
    cells = levels * lat_rows * lon
    heads, entries = earth_bias.shape[-2:]
    slabs = lon // WW
    half_cells = cells // slabs
    hidden = expand_weight.shape[2]
    wide = -(-(width + 2) // 128) * 128
    lines = -(-heads * GROUP // 8) * 8
    tiles = cells // 16
    edges = (0, tiles // 2 * 16, (tiles - tiles // 6) * 16, cells)
    chunks = len(edges) - 1
    lanes = -(-WZ * WH * (2 * WW - 1) // 128) * 128
    q_weight, p_weight = qkv_weight[0].T, proj_weight[0].T
    vmem = pl.BlockSpec(memory_space=pltpu.VMEM)
    dma = pltpu.SemaphoreType.DMA
    out = pl.pallas_call(
        functools.partial(kernel, tp, micro, heads, slabs, edges),
        out_shape=jax.ShapeDtypeStruct((micro, cells, width), BF16),
        in_specs=[pl.BlockSpec(memory_space=pltpu.HBM)] * 14,
        out_specs=vmem,
        scratch_shapes=[
            pltpu.VMEM((micro, cells, width), BF16),
            pltpu.VMEM((1, width), BF16),
            pltpu.VMEM((1, width), BF16),
            pltpu.VMEM(q_weight.shape, BF16),
            pltpu.VMEM(qkv_bias.shape, BF16),
            pltpu.VMEM(p_weight.shape, BF16),
            pltpu.VMEM(proj_bias.shape, BF16),
            pltpu.VMEM((1, width), BF16),
            pltpu.VMEM((1, width), BF16),
            pltpu.VMEM((width, hidden), BF16),
            pltpu.VMEM((1, hidden), BF16),
            pltpu.VMEM(reduce_bias.shape, BF16),
            pltpu.VMEM((heads, 1, entries), F32),
            pltpu.VMEM((3 * width, wide), BF16),
            pltpu.VMEM((width, wide), BF16),
            pltpu.VMEM((tp * hidden, wide), BF16),
            pltpu.VMEM((tp * hidden, width), BF16),
            pltpu.VMEM((micro, cells, width), BF16),
            pltpu.VMEM((micro, 2, cells, width), BF16),
            pltpu.VMEM((micro, cells, width), BF16),
            pltpu.VMEM((cells, cells), BF16),
            pltpu.VMEM((cells, cells), BF16),
            pltpu.VMEM((cells, wide), BF16),
            pltpu.VMEM((cells, wide), BF16),
            pltpu.VMEM((cells, wide), BF16),
            pltpu.VMEM((lines, lanes), F32),
            pltpu.VMEM((heads * half_cells, 2 * half_cells), F32),
            pltpu.VMEM((2 * half_cells, heads * half_cells), F32),
            dma((14,)),
            dma((4, 3)),
            dma((4, 3)),
            dma,
            dma,
            dma((micro, 2, chunks)),
            dma((micro, 2, chunks)),
        ],
        compiler_params=pltpu.CompilerParams(
            collective_id=0, has_side_effects=True, vmem_limit_bytes=60 * 1024 * 1024),
    )(
        initial_field.reshape(micro, cells, width), first_gain, first_shift, q_weight, qkv_bias,
        p_weight, proj_bias, second_gain, second_shift, expand_weight[0], expand_bias,
        reduce_weight[0], reduce_bias, earth_bias.reshape(heads, 1, entries),
    )
    return out.reshape(1, micro, levels, lat_rows, lon, width)


def solution(mesh):
    return jax.shard_map(
        on_device,
        mesh=mesh,
        in_specs=(
            P(None, "tp", "lat", None, None),
            P("section", None),
            P("section", None),
            P("section", None, "tp"),
            P("section", "tp"),
            P("section", None, "tp"),
            P("section", "tp"),
            P("section", None),
            P("section", None),
            P("section", None, "tp"),
            P("section", "tp"),
            P("section", "tp", None),
            P("section", "tp"),
            P("section", "tp", "lat", None, None),
        ),
        out_specs=P("section", None, "tp", "lat", None, None),
        check_vma=False,
    )
```

```python
import functools

import jax
import jax.numpy as jnp
import numpy as np
from jax import lax
from jax.experimental import pallas as pl
from jax.experimental.pallas import tpu as pltpu
from jax.sharding import PartitionSpec as P

WZ = 2
WH = 6
WW = 12
HALF = WH // 2
GROUP = WZ * HALF
EPS = 1e-05
MESH = pl.DeviceIdType.MESH
F32 = jnp.float32
BF16 = jnp.bfloat16
NT = (((1,), (1,)), ((), ()))
TN = (((0,), (0,)), ((), ()))
LOG2E = float(np.log2(np.e))


def mm(a, b):
    return jnp.dot(a, b, preferred_element_type=F32)


def mm_nt(a, b):
    return lax.dot_general(a, b, NT, preferred_element_type=F32)


def layer_norm(values, gain, shift):
    mean = jnp.mean(values, axis=-1, keepdims=True)
    centred = values - mean
    spread = jnp.mean(centred * centred, axis=-1, keepdims=True)
    return centred * lax.rsqrt(spread + EPS) * gain + shift


def kernel(
    tp, heads, slabs, edges,
    x_in, g1_in, s1_in, qw_in, qb_in, pw_in, pb_in, g2_in, s2_in,
    ew_in, eb_in, rw_in, rb_in, table_in,
    out_ref,
    x_ref, g1_ref, s1_ref, qw_ref, qb_ref, pw_ref, pb_ref, g2_ref, s2_ref,
    ew_ref, eb_ref, rb_ref, tables,
    qkv, proj, expand, reduce, norms, near_raw, near_mid, outp, foreign, perm, unperm,
    own_n, near_n, att_n, table, spread, bias,
    l_sem, w_send, w_recv, f_send, f_recv, n_send, n_recv, o_send, o_recv,
):
    me = lax.axis_index("tp")
    lat = lax.axis_index("lat")
    section = lax.axis_index("section")
    pair = lat + 1 - 2 * lax.rem(lat, 2)
    other = 1 - section
    cells, width = x_ref.shape
    wide = own_n.shape[1]
    half_cells = cells // slabs
    head_size = width // heads
    q_part, p_part, e_part = qw_ref.shape[0], pw_ref.shape[0], ew_ref.shape[1]
    core_peer = me + 1 - 2 * lax.rem(me, 2)
    chip_peer = lax.rem(me + tp // 2, tp)

    barrier = pltpu.get_barrier_semaphore()
    pl.semaphore_signal(barrier, inc=1, device_id={"tp": core_peer}, device_id_type=MESH)
    pl.semaphore_signal(barrier, inc=1, device_id={"tp": chip_peer}, device_id_type=MESH)
    pl.semaphore_signal(barrier, inc=1, device_id={"lat": pair}, device_id_type=MESH)
    pl.semaphore_signal(barrier, inc=1, device_id={"section": other}, device_id_type=MESH)

    def owner_rows(owner, part):
        return pl.ds(pl.multiple_of(owner * part, 16), part)

    loads = [
        pltpu.make_async_copy(source, target, l_sem.at[n])
        for n, (source, target) in enumerate((
            (qw_in, qw_ref), (qb_in, qb_ref), (pw_in, pw_ref), (pb_in, pb_ref), (rb_in, rb_ref),
            (ew_in, ew_ref), (eb_in, eb_ref), (rw_in, reduce.at[section, owner_rows(me, e_part), :]),
            (g1_in, g1_ref), (s1_in, s1_ref), (g2_in, g2_ref), (s2_in, s2_ref),
            (x_in.at[section], x_ref), (table_in, tables.at[section]),
        ))
    ]
    for load in loads:
        load.start()

    for load in loads[:5]:
        load.wait()
    tail = lax.broadcasted_iota(jnp.int32, (wide - width, q_part), 0)
    q_tail = jnp.where(tail == 0, qb_ref[...].astype(F32), 0.0).T
    qkv[section, owner_rows(me, q_part), :] = jnp.concatenate(
        [qw_ref[...].astype(F32), q_tail], axis=1).astype(BF16)
    tail = lax.broadcasted_iota(jnp.int32, (wide - width, p_part), 0)
    p_tail = jnp.where(
        tail == 0, pb_ref[...].astype(F32), jnp.where(tail == 1, rb_ref[...].astype(F32), 0.0)).T
    proj[section, owner_rows(me, p_part), :] = jnp.concatenate(
        [pw_ref[...].astype(F32), p_tail], axis=1).astype(BF16)
    for load in loads[5:12]:
        load.wait()
    tail = lax.broadcasted_iota(jnp.int32, (wide - width, e_part), 0)
    expand[section, owner_rows(me, e_part), :] = jnp.concatenate(
        [ew_ref[...].astype(F32), jnp.where(tail == 0, eb_ref[...].astype(F32), 0.0)], axis=0).T.astype(BF16)
    line = lax.broadcasted_iota(jnp.int32, (16, width), 0)
    packed = jnp.where(line == 0, g1_ref[...].astype(F32), s1_ref[...].astype(F32))
    packed = jnp.where(line == 2, g2_ref[...].astype(F32), packed)
    norms[section] = jnp.where(line == 3, s2_ref[...].astype(F32), packed).astype(BF16)

    pl.semaphore_wait(barrier, 4)

    def weight_copy(model, kind, way):
        owner = chip_peer if way == 2 else me
        target = (
            lambda: qkv.at[model, owner_rows(owner, q_part), :],
            lambda: proj.at[model, owner_rows(owner, p_part), :],
            lambda: expand.at[model, owner_rows(owner, e_part), :],
            lambda: reduce.at[model, owner_rows(owner, e_part), :],
            lambda: norms.at[model],
            lambda: tables.at[model],
        )[kind]()
        device = ({"tp": core_peer}, {"tp": chip_peer}, {"tp": core_peer}, {"section": other})[way]
        return pltpu.make_async_remote_copy(
            src_ref=table_in if kind == 5 else target, dst_ref=target,
            send_sem=w_send.at[model, kind, way], recv_sem=w_recv.at[model, kind, way],
            device_id=device, device_id_type=MESH)

    def share_out(model, kind):
        @pl.when(section != model)
        def _():
            weight_copy(model, kind, 3).wait_recv()

        weight_copy(model, kind, 1).start()
        weight_copy(model, kind, 0).start()

    def hand_on(model, kind):
        weight_copy(model, kind, 1).wait_recv()
        weight_copy(model, kind, 2).start()

    def weights_here(model, kind):
        weight_copy(model, kind, 0).wait_recv()
        weight_copy(model, kind, 2).wait_recv()

    field_copy = pltpu.make_async_remote_copy(
        src_ref=x_in.at[section], dst_ref=near_raw, send_sem=f_send, recv_sem=f_recv,
        device_id={"lat": pair}, device_id_type=MESH)
    chunks = len(edges) - 1

    def pair_copy(part):
        rows = pl.ds(edges[part], edges[part + 1] - edges[part])
        return pltpu.make_async_remote_copy(
            src_ref=outp.at[0, rows], dst_ref=near_mid.at[rows], send_sem=n_send.at[part],
            recv_sem=n_recv.at[part], device_id={"lat": pair}, device_id_type=MESH)

    def result_copy(model, part):
        rows = pl.ds(edges[part], edges[part + 1] - edges[part])
        return pltpu.make_async_remote_copy(
            src_ref=outp.at[model, rows], dst_ref=foreign.at[rows], send_sem=o_send.at[part],
            recv_sem=o_recv.at[part], device_id={"section": other}, device_id_type=MESH)

    weight_copy(section, 0, 3).start()

    @pl.when(section == 0)
    def _():
        weight_copy(0, 0, 1).start()
        weight_copy(0, 0, 0).start()

    field_copy.start()
    for kind in (5, 4, 1, 2, 3):
        weight_copy(section, kind, 3).start()

    @pl.when(section == 0)
    def _():
        for kind in (1, 2, 3):
            weight_copy(0, kind, 1).start()
            weight_copy(0, kind, 0).start()

    def share_on(kind):
        @pl.when(section == 1)
        def _():
            weight_copy(0, kind, 3).wait_recv()
            weight_copy(0, kind, 1).start()
            weight_copy(0, kind, 0).start()

    for load in loads[12:]:
        load.wait()

    stretch = cells // GROUP
    step = -(-65536 // GROUP)
    line = lax.broadcasted_iota(jnp.int32, (1, cells), 1)
    level_row = sum((line >= stretch * k).astype(jnp.int32) for k in range(1, GROUP))
    forth = (line - stretch * level_row) * GROUP + level_row
    column = lax.shift_right_logical(line * step, 16)
    back = (line - GROUP * column) * stretch + column
    rows = lax.broadcasted_iota(jnp.int32, (cells, cells), 0)
    perm[...] = (rows == forth).astype(F32).astype(BF16)
    unperm[...] = (rows == back).astype(F32).astype(BF16)
    lanes = lax.broadcasted_iota(jnp.int32, (cells, wide), 1)
    ones = (lanes == width).astype(F32).astype(BF16)
    own_n[...] = ones
    near_n[...] = ones
    att_n[...] = ones
    own_field = mm(perm[...], x_ref[...])

    span = WH * (2 * WW - 1)
    c = lax.broadcasted_iota(jnp.int32, (1, 2 * half_cells), 1)
    far = (c >= half_cells).astype(jnp.int32)
    c = c - half_cells * far
    wk = sum((c >= GROUP * k).astype(jnp.int32) for k in range(1, WW))
    zr = c - GROUP * wk
    zk = (zr >= HALF).astype(jnp.int32)
    band = lax.rem(lat, 2)
    hk = zr - HALF * zk + HALF * (band + far - 2 * band * far)
    place = zk * span + hk * (2 * WW - 1) + WW - 1 - wk
    pick = (lax.broadcasted_iota(jnp.int32, (table.shape[1], 2 * half_cells), 0) == place).astype(F32).astype(BF16)
    table[...] = jnp.zeros_like(table)

    def expand_bias(model):
        for zq in range(WZ):
            for zk in range(WZ):
                for r in range(HALF):
                    off = ((zq * WZ + zk) * HALF + r) * span
                    piece = tables[model, :, 0, off:off + span]
                    for h in range(heads):
                        row = h * GROUP + zq * HALF + r
                        table[row:row + 1, zk * span:(zk + 1) * span] = piece[h:h + 1]
        full = table[...]
        lines = full.shape[0]
        turned = jnp.concatenate(
            [full if wq == 0 else pltpu.roll(full, full.shape[1] - wq, 1) for wq in range(WW)], axis=0)
        first = turned.astype(BF16)
        rest = turned - first.astype(F32)
        second = rest.astype(BF16)
        third = (rest - second.astype(F32)).astype(BF16)
        total = mm(first, pick) + mm(second, pick) + mm(third, pick)
        for wq in range(WW):
            for h in range(heads):
                at, row = h * half_cells + wq * GROUP, wq * lines + h * GROUP
                spread[at:at + GROUP, :] = total[row:row + GROUP]
        bias[...] = spread[...].T * LOG2E

    share_on(0)
    share_on(1)

    scale = LOG2E / float(np.sqrt(head_size))
    lane_head = lax.broadcasted_iota(jnp.int32, (half_cells, width), 1)
    in_head = [(lane_head >= h * head_size) & (lane_head < (h + 1) * head_size) for h in range(heads)]

    for model in range(2):
        @pl.when(section != model)
        def _():
            weight_copy(model, 4, 3).wait_recv()
            weight_copy(model, 5, 3).wait_recv()

        expand_bias(model)
        g1, s1, g2, s2 = (norms[model, n:n + 1, :].astype(F32) for n in range(4))
        hand_on(model, 0)
        grid = own_field if model == 0 else outp[0].astype(F32)
        own_n[:, :width] = layer_norm(grid, g1, s1).astype(BF16)
        if model == 0:
            share_on(2)
        hand_on(model, 1)
        weights_here(model, 0)
        q = mm_nt(own_n[...], qkv[model, :width, :])
        k_own = mm_nt(own_n[...], qkv[model, width:2 * width, :])
        v_own = mm_nt(own_n[...], qkv[model, 2 * width:, :])
        if model == 0:
            field_copy.wait_recv()
            near = mm(perm[...], near_raw[...])
        else:
            for part in range(chunks):
                pair_copy(part).wait_recv()
            near = near_mid[...].astype(F32)
        near_n[:, :width] = layer_norm(near, g1, s1).astype(BF16)
        k_near = mm_nt(near_n[...], qkv[model, width:2 * width, :])
        v_near = mm_nt(near_n[...], qkv[model, 2 * width:, :])
        if model == 0:
            share_on(3)
        attended = []
        for s in range(slabs):
            cut = slice(s * half_cells, (s + 1) * half_cells)
            keys = jnp.concatenate([k_own[cut], k_near[cut]], axis=0).astype(BF16)
            vals = jnp.concatenate([v_own[cut], v_near[cut]], axis=0).astype(BF16)
            stack = jnp.concatenate([jnp.where(m, q[cut], 0.0) for m in in_head], axis=0).astype(BF16)
            scores = mm_nt(keys, stack) * scale + bias[...]
            e = jnp.exp2(scores - jnp.max(scores, axis=0, keepdims=True))
            probs = (e * (1.0 / jnp.sum(e, axis=0, keepdims=True))).astype(BF16)
            mixed = lax.dot_general(probs, vals, TN, preferred_element_type=F32)
            total = jnp.zeros((half_cells, width), F32)
            for h, m in enumerate(in_head):
                total = jnp.where(m, mixed[h * half_cells:(h + 1) * half_cells], total)
            attended.append(total)
        att_n[:, :width] = jnp.concatenate(attended, axis=0).astype(BF16)
        hand_on(model, 2)
        hand_on(model, 3)
        weights_here(model, 1)
        middle = (grid + mm_nt(att_n[...], proj[model])).astype(BF16).astype(F32)
        pick_row = (lax.broadcasted_iota(jnp.int32, (16, wide), 1) == width + 1).astype(F32).astype(BF16)
        shift_out = mm_nt(pick_row, proj[model])[:1]
        own_n[:, :width] = layer_norm(middle, g2, s2).astype(BF16)
        if model == 0:
            for kind in range(4):
                share_out(1, kind)
        weights_here(model, 2)
        for part in range(chunks):
            cut = slice(edges[part], edges[part + 1])
            pre = mm_nt(own_n[cut, :], expand[model])
            hidden = (0.5 * pre * (1.0 + lax.erf(pre * float(np.sqrt(0.5))))).astype(BF16)
            if part == 0:
                weights_here(model, 3)
            result = middle[cut] + shift_out + mm(hidden, reduce[model])
            outp[model, cut, :] = result.astype(BF16)
            if model == 0:
                pair_copy(part).start()

            @pl.when(section != model)
            def _():
                result_copy(model, part).start()

    @pl.when(section == 0)
    def _():
        out_ref[0] = mm(unperm[...], outp[0]).astype(BF16)

    @pl.when(section == 1)
    def _():
        out_ref[1] = mm(unperm[...], outp[1]).astype(BF16)

    for part in range(chunks):
        result_copy(other, part).wait_recv()
    out_ref[other] = mm(unperm[...], foreign[...]).astype(BF16)

    for kind in range(6):
        weight_copy(section, kind, 3).wait_send()
    for model in range(2):
        for kind in range(4):
            for way in range(3):
                weight_copy(model, kind, way).wait_send()
    field_copy.wait_send()
    for part in range(chunks):
        pair_copy(part).wait_send()
        result_copy(other, part).wait_send()


def on_device(
    initial_field, first_gain, first_shift, qkv_weight, qkv_bias, proj_weight, proj_bias,
    second_gain, second_shift, expand_weight, expand_bias, reduce_weight, reduce_bias, earth_bias,
):
    tp = lax.axis_size("tp")
    micro, levels, lat_rows, lon, width = initial_field.shape
    cells = levels * lat_rows * lon
    heads, entries = earth_bias.shape[-2:]
    slabs = lon // WW
    half_cells = cells // slabs
    hidden = expand_weight.shape[2]
    wide = -(-(width + 2) // 128) * 128
    lines = -(-heads * GROUP // 8) * 8
    tiles = cells // 16
    edges = (0, tiles // 2 * 16, (tiles - tiles // 6) * 16, cells)
    chunks = len(edges) - 1
    lanes = -(-WZ * WH * (2 * WW - 1) // 128) * 128
    q_weight, p_weight = qkv_weight[0].T, proj_weight[0].T
    vmem = pl.BlockSpec(memory_space=pltpu.VMEM)
    dma = pltpu.SemaphoreType.DMA
    out = pl.pallas_call(
        functools.partial(kernel, tp, heads, slabs, edges),
        out_shape=jax.ShapeDtypeStruct((micro, cells, width), BF16),
        in_specs=[pl.BlockSpec(memory_space=pltpu.HBM)] * 14,
        out_specs=vmem,
        scratch_shapes=[
            pltpu.VMEM((cells, width), BF16),
            pltpu.VMEM((1, width), BF16),
            pltpu.VMEM((1, width), BF16),
            pltpu.VMEM(q_weight.shape, BF16),
            pltpu.VMEM(qkv_bias.shape, BF16),
            pltpu.VMEM(p_weight.shape, BF16),
            pltpu.VMEM(proj_bias.shape, BF16),
            pltpu.VMEM((1, width), BF16),
            pltpu.VMEM((1, width), BF16),
            pltpu.VMEM((width, hidden), BF16),
            pltpu.VMEM((1, hidden), BF16),
            pltpu.VMEM(reduce_bias.shape, BF16),
            pltpu.VMEM((2, heads, 1, entries), F32),
            pltpu.VMEM((2, 3 * width, wide), BF16),
            pltpu.VMEM((2, width, wide), BF16),
            pltpu.VMEM((2, tp * hidden, wide), BF16),
            pltpu.VMEM((2, tp * hidden, width), BF16),
            pltpu.VMEM((2, 16, width), BF16),
            pltpu.VMEM((cells, width), BF16),
            pltpu.VMEM((cells, width), BF16),
            pltpu.VMEM((2, cells, width), BF16),
            pltpu.VMEM((cells, width), BF16),
            pltpu.VMEM((cells, cells), BF16),
            pltpu.VMEM((cells, cells), BF16),
            pltpu.VMEM((cells, wide), BF16),
            pltpu.VMEM((cells, wide), BF16),
            pltpu.VMEM((cells, wide), BF16),
            pltpu.VMEM((lines, lanes), F32),
            pltpu.VMEM((heads * half_cells, 2 * half_cells), F32),
            pltpu.VMEM((2 * half_cells, heads * half_cells), F32),
            dma((14,)),
            dma((2, 6, 4)),
            dma((2, 6, 4)),
            dma,
            dma,
            dma((chunks,)),
            dma((chunks,)),
            dma((chunks,)),
            dma((chunks,)),
        ],
        compiler_params=pltpu.CompilerParams(
            collective_id=0, has_side_effects=True, vmem_limit_bytes=60 * 1024 * 1024),
    )(
        initial_field.reshape(micro, cells, width), first_gain, first_shift, q_weight, qkv_bias,
        p_weight, proj_bias, second_gain, second_shift, expand_weight[0], expand_bias,
        reduce_weight[0], reduce_bias, earth_bias.reshape(heads, 1, entries),
    )
    return out.reshape(1, micro, levels, lat_rows, lon, width)


def solution(mesh):
    return jax.shard_map(
        on_device,
        mesh=mesh,
        in_specs=(
            P(None, "tp", "lat", None, None),
            P("section", None),
            P("section", None),
            P("section", None, "tp"),
            P("section", "tp"),
            P("section", None, "tp"),
            P("section", "tp"),
            P("section", None),
            P("section", None),
            P("section", None, "tp"),
            P("section", "tp"),
            P("section", "tp", None),
            P("section", "tp"),
            P("section", "tp", "lat", None, None),
        ),
        out_specs=P("section", None, "tp", "lat", None, None),
        check_vma=False,
    )
```

```python
import functools

import jax
import jax.numpy as jnp
import numpy as np
from jax import lax
from jax.experimental import pallas as pl
from jax.experimental.pallas import tpu as pltpu
from jax.sharding import PartitionSpec as P

WZ = 2
WH = 6
WW = 12
HALF = WH // 2
GROUP = WZ * HALF
EPS = 1e-05
MESH = pl.DeviceIdType.MESH
F32 = jnp.float32
BF16 = jnp.bfloat16
NT = (((1,), (1,)), ((), ()))
TN = (((0,), (0,)), ((), ()))
LOG2E = float(np.log2(np.e))


def mm(a, b):
    return jnp.dot(a, b, preferred_element_type=F32)


def mm_nt(a, b):
    return lax.dot_general(a, b, NT, preferred_element_type=F32)


def layer_norm(values, gain, shift):
    mean = jnp.mean(values, axis=-1, keepdims=True)
    centred = values - mean
    spread = jnp.mean(centred * centred, axis=-1, keepdims=True)
    return centred * lax.rsqrt(spread + EPS) * gain + shift


def kernel(
    tp, heads, slabs, edges,
    x_in, g1_in, s1_in, qw_in, qb_in, pw_in, pb_in, g2_in, s2_in,
    ew_in, eb_in, rw_in, rb_in, table_in,
    out_ref,
    x_ref, g1_ref, s1_ref, qw_ref, qb_ref, pw_ref, pb_ref, g2_ref, s2_ref,
    ew_ref, eb_ref, rb_ref, tables,
    qkv, proj, expand, reduce, norms, near_raw, near_mid, outp, foreign, perm, unperm,
    own_n, near_n, att_n, table, spread, bias,
    l_sem, w_send, w_recv, f_send, f_recv, n_send, n_recv, o_send, o_recv,
):
    me = lax.axis_index("tp")
    lat = lax.axis_index("lat")
    section = lax.axis_index("section")
    pair = lat + 1 - 2 * lax.rem(lat, 2)
    other = 1 - section
    cells, width = x_ref.shape
    wide = own_n.shape[1]
    half_cells = cells // slabs
    head_size = width // heads
    q_part, p_part, e_part = qw_ref.shape[0], pw_ref.shape[0], ew_ref.shape[1]
    core_peer = me + 1 - 2 * lax.rem(me, 2)
    chip_peer = lax.rem(me + tp // 2, tp)

    barrier = pltpu.get_barrier_semaphore()
    pl.semaphore_signal(barrier, inc=1, device_id={"tp": core_peer}, device_id_type=MESH)
    pl.semaphore_signal(barrier, inc=1, device_id={"tp": chip_peer}, device_id_type=MESH)
    pl.semaphore_signal(barrier, inc=1, device_id={"lat": pair}, device_id_type=MESH)
    pl.semaphore_signal(barrier, inc=1, device_id={"section": other}, device_id_type=MESH)

    def owner_rows(owner, part):
        return pl.ds(pl.multiple_of(owner * part, 16), part)

    loads = [
        pltpu.make_async_copy(source, target, l_sem.at[n])
        for n, (source, target) in enumerate((
            (qw_in, qw_ref), (qb_in, qb_ref), (pw_in, pw_ref), (pb_in, pb_ref), (rb_in, rb_ref),
            (ew_in, ew_ref), (eb_in, eb_ref), (rw_in, reduce.at[section, owner_rows(me, e_part), :]),
            (g1_in, g1_ref), (s1_in, s1_ref), (g2_in, g2_ref), (s2_in, s2_ref),
            (x_in.at[section], x_ref), (table_in, tables.at[section]),
        ))
    ]
    for load in loads:
        load.start()

    for load in loads[:2]:
        load.wait()
    tail = lax.broadcasted_iota(jnp.int32, (wide - width, q_part), 0)
    q_tail = jnp.where(tail == 0, qb_ref[...].astype(F32), 0.0).T
    qkv[section, owner_rows(me, q_part), :] = jnp.concatenate(
        [qw_ref[...].astype(F32), q_tail], axis=1).astype(BF16)
    pl.semaphore_wait(barrier, 4)

    def weight_copy(model, kind, way):
        owner = chip_peer if way == 2 else me
        target = (
            lambda: qkv.at[model, owner_rows(owner, q_part), :],
            lambda: proj.at[model, owner_rows(owner, p_part), :],
            lambda: expand.at[model, owner_rows(owner * 2, e_part // 2), :],
            lambda: expand.at[model, owner_rows(owner * 2 + 1, e_part // 2), :],
            lambda: reduce.at[model, owner_rows(owner * 2, e_part // 2), :],
            lambda: reduce.at[model, owner_rows(owner * 2 + 1, e_part // 2), :],
            lambda: norms.at[model],
            lambda: tables.at[model],
        )[kind]()
        device = ({"tp": core_peer}, {"tp": chip_peer}, {"tp": core_peer}, {"section": other})[way]
        return pltpu.make_async_remote_copy(
            src_ref=table_in if kind == 7 else target, dst_ref=target,
            send_sem=w_send.at[model, kind, way], recv_sem=w_recv.at[model, kind, way],
            device_id=device, device_id_type=MESH)

    def share_out(model, kind):
        @pl.when(section != model)
        def _():
            weight_copy(model, kind, 3).wait_recv()

        weight_copy(model, kind, 1).start()
        weight_copy(model, kind, 0).start()

    def hand_on(model, kind):
        weight_copy(model, kind, 1).wait_recv()
        weight_copy(model, kind, 2).start()

    def weights_here(model, kind):
        weight_copy(model, kind, 0).wait_recv()
        weight_copy(model, kind, 2).wait_recv()

    field_copy = pltpu.make_async_remote_copy(
        src_ref=x_in.at[section], dst_ref=near_raw, send_sem=f_send, recv_sem=f_recv,
        device_id={"lat": pair}, device_id_type=MESH)
    chunks = len(edges) - 1

    def pair_copy(part):
        rows = pl.ds(edges[part], edges[part + 1] - edges[part])
        return pltpu.make_async_remote_copy(
            src_ref=outp.at[0, rows], dst_ref=near_mid.at[rows], send_sem=n_send.at[part],
            recv_sem=n_recv.at[part], device_id={"lat": pair}, device_id_type=MESH)

    def result_copy(model, part):
        rows = pl.ds(edges[part], edges[part + 1] - edges[part])
        return pltpu.make_async_remote_copy(
            src_ref=outp.at[model, rows], dst_ref=foreign.at[rows], send_sem=o_send.at[part],
            recv_sem=o_recv.at[part], device_id={"section": other}, device_id_type=MESH)

    def own_shares(*kinds):
        for kind in kinds:
            weight_copy(section, kind, 3).start()

        @pl.when(section == 0)
        def _():
            for kind in kinds:
                if kind < 6:
                    weight_copy(0, kind, 1).start()
                    weight_copy(0, kind, 0).start()

    own_shares(0, 7)
    field_copy.start()
    for load in loads[2:5]:
        load.wait()
    tail = lax.broadcasted_iota(jnp.int32, (wide - width, p_part), 0)
    p_tail = jnp.where(
        tail == 0, pb_ref[...].astype(F32), jnp.where(tail == 1, rb_ref[...].astype(F32), 0.0)).T
    proj[section, owner_rows(me, p_part), :] = jnp.concatenate(
        [pw_ref[...].astype(F32), p_tail], axis=1).astype(BF16)
    for load in loads[5:12]:
        load.wait()
    line = lax.broadcasted_iota(jnp.int32, (16, width), 0)
    packed = jnp.where(line == 0, g1_ref[...].astype(F32), s1_ref[...].astype(F32))
    packed = jnp.where(line == 2, g2_ref[...].astype(F32), packed)
    norms[section] = jnp.where(line == 3, s2_ref[...].astype(F32), packed).astype(BF16)
    own_shares(6, 1)
    tail = lax.broadcasted_iota(jnp.int32, (wide - width, e_part), 0)
    expand[section, owner_rows(me, e_part), :] = jnp.concatenate(
        [ew_ref[...].astype(F32), jnp.where(tail == 0, eb_ref[...].astype(F32), 0.0)], axis=0).T.astype(BF16)
    own_shares(2, 3, 4, 5)

    def share_on(kind):
        @pl.when(section == 1)
        def _():
            weight_copy(0, kind, 3).wait_recv()
            weight_copy(0, kind, 1).start()
            weight_copy(0, kind, 0).start()

    for load in loads[12:]:
        load.wait()

    stretch = cells // GROUP
    step = -(-65536 // GROUP)
    line = lax.broadcasted_iota(jnp.int32, (1, cells), 1)
    level_row = sum((line >= stretch * k).astype(jnp.int32) for k in range(1, GROUP))
    forth = (line - stretch * level_row) * GROUP + level_row
    column = lax.shift_right_logical(line * step, 16)
    back = (line - GROUP * column) * stretch + column
    rows = lax.broadcasted_iota(jnp.int32, (cells, cells), 0)
    perm[...] = (rows == forth).astype(F32).astype(BF16)
    unperm[...] = (rows == back).astype(F32).astype(BF16)
    lanes = lax.broadcasted_iota(jnp.int32, (cells, wide), 1)
    ones = (lanes == width).astype(F32).astype(BF16)
    own_n[...] = ones
    near_n[...] = ones
    att_n[...] = ones
    own_field = mm(perm[...], x_ref[...])

    span = WH * (2 * WW - 1)
    c = lax.broadcasted_iota(jnp.int32, (1, 2 * half_cells), 1)
    far = (c >= half_cells).astype(jnp.int32)
    c = c - half_cells * far
    wk = sum((c >= GROUP * k).astype(jnp.int32) for k in range(1, WW))
    zr = c - GROUP * wk
    zk = (zr >= HALF).astype(jnp.int32)
    band = lax.rem(lat, 2)
    hk = zr - HALF * zk + HALF * (band + far - 2 * band * far)
    place = zk * span + hk * (2 * WW - 1) + WW - 1 - wk
    pick = (lax.broadcasted_iota(jnp.int32, (table.shape[1], 2 * half_cells), 0) == place).astype(F32).astype(BF16)
    table[...] = jnp.zeros_like(table)

    def expand_bias(model):
        for zq in range(WZ):
            for zk in range(WZ):
                for r in range(HALF):
                    off = ((zq * WZ + zk) * HALF + r) * span
                    piece = tables[model, :, 0, off:off + span]
                    for h in range(heads):
                        row = h * GROUP + zq * HALF + r
                        table[row:row + 1, zk * span:(zk + 1) * span] = piece[h:h + 1]
        full = table[...]
        lines = full.shape[0]
        turned = jnp.concatenate(
            [full if wq == 0 else pltpu.roll(full, full.shape[1] - wq, 1) for wq in range(WW)], axis=0)
        first = turned.astype(BF16)
        rest = turned - first.astype(F32)
        second = rest.astype(BF16)
        third = (rest - second.astype(F32)).astype(BF16)
        total = mm(first, pick) + mm(second, pick) + mm(third, pick)
        for wq in range(WW):
            for h in range(heads):
                at, row = h * half_cells + wq * GROUP, wq * lines + h * GROUP
                spread[at:at + GROUP, :] = total[row:row + GROUP]
        bias[...] = spread[...].T * LOG2E

    share_on(0)
    share_on(1)

    scale = LOG2E / float(np.sqrt(head_size))
    lane_head = lax.broadcasted_iota(jnp.int32, (half_cells, width), 1)
    in_head = [(lane_head >= h * head_size) & (lane_head < (h + 1) * head_size) for h in range(heads)]

    for model in range(2):
        @pl.when(section != model)
        def _():
            weight_copy(model, 6, 3).wait_recv()
            weight_copy(model, 7, 3).wait_recv()

        expand_bias(model)
        g1, s1, g2, s2 = (norms[model, n:n + 1, :].astype(F32) for n in range(4))
        hand_on(model, 0)
        grid = own_field if model == 0 else outp[0].astype(F32)
        own_n[:, :width] = layer_norm(grid, g1, s1).astype(BF16)
        if model == 0:
            share_on(2)
            share_on(3)
        hand_on(model, 1)
        weights_here(model, 0)
        q = mm_nt(own_n[...], qkv[model, :width, :])
        k_own = mm_nt(own_n[...], qkv[model, width:2 * width, :])
        v_own = mm_nt(own_n[...], qkv[model, 2 * width:, :])
        if model == 0:
            field_copy.wait_recv()
            near = mm(perm[...], near_raw[...])
        else:
            for part in range(chunks):
                pair_copy(part).wait_recv()
            near = near_mid[...].astype(F32)
        near_n[:, :width] = layer_norm(near, g1, s1).astype(BF16)
        k_near = mm_nt(near_n[...], qkv[model, width:2 * width, :])
        v_near = mm_nt(near_n[...], qkv[model, 2 * width:, :])
        if model == 0:
            share_on(4)
            share_on(5)
        attended = []
        for s in range(slabs):
            cut = slice(s * half_cells, (s + 1) * half_cells)
            keys = jnp.concatenate([k_own[cut], k_near[cut]], axis=0).astype(BF16)
            vals = jnp.concatenate([v_own[cut], v_near[cut]], axis=0).astype(BF16)
            stack = jnp.concatenate([jnp.where(m, q[cut], 0.0) for m in in_head], axis=0).astype(BF16)
            scores = mm_nt(keys, stack) * scale + bias[...]
            e = jnp.exp2(scores - jnp.max(scores, axis=0, keepdims=True))
            probs = (e * (1.0 / jnp.sum(e, axis=0, keepdims=True))).astype(BF16)
            mixed = lax.dot_general(probs, vals, TN, preferred_element_type=F32)
            total = jnp.zeros((half_cells, width), F32)
            for h, m in enumerate(in_head):
                total = jnp.where(m, mixed[h * half_cells:(h + 1) * half_cells], total)
            attended.append(total)
        att_n[:, :width] = jnp.concatenate(attended, axis=0).astype(BF16)
        hand_on(model, 2)
        weights_here(model, 1)
        middle = (grid + mm_nt(att_n[...], proj[model])).astype(BF16).astype(F32)
        pick_row = (lax.broadcasted_iota(jnp.int32, (16, wide), 1) == width + 1).astype(F32).astype(BF16)
        shift_out = mm_nt(pick_row, proj[model])[:1]
        own_n[:, :width] = layer_norm(middle, g2, s2).astype(BF16)
        for kind in (3, 4, 5):
            hand_on(model, kind)
        if model == 0:
            for kind in range(6):
                share_out(1, kind)
        weights_here(model, 2)
        weights_here(model, 3)
        for part in range(chunks):
            cut = slice(edges[part], edges[part + 1])
            pre = mm_nt(own_n[cut, :], expand[model])
            hidden = (0.5 * pre * (1.0 + lax.erf(pre * float(np.sqrt(0.5))))).astype(BF16)
            if part == 0:
                weights_here(model, 4)
                weights_here(model, 5)
            result = middle[cut] + shift_out + mm(hidden, reduce[model])
            outp[model, cut, :] = result.astype(BF16)
            if model == 0:
                pair_copy(part).start()

            @pl.when(section != model)
            def _():
                result_copy(model, part).start()

    @pl.when(section == 0)
    def _():
        out_ref[0] = mm(unperm[...], outp[0]).astype(BF16)

    @pl.when(section == 1)
    def _():
        out_ref[1] = mm(unperm[...], outp[1]).astype(BF16)

    for part in range(chunks):
        result_copy(other, part).wait_recv()
    out_ref[other] = mm(unperm[...], foreign[...]).astype(BF16)

    for kind in range(8):
        weight_copy(section, kind, 3).wait_send()
    for model in range(2):
        for kind in range(6):
            for way in range(3):
                weight_copy(model, kind, way).wait_send()
    field_copy.wait_send()
    for part in range(chunks):
        pair_copy(part).wait_send()
        result_copy(other, part).wait_send()


def on_device(
    initial_field, first_gain, first_shift, qkv_weight, qkv_bias, proj_weight, proj_bias,
    second_gain, second_shift, expand_weight, expand_bias, reduce_weight, reduce_bias, earth_bias,
):
    tp = lax.axis_size("tp")
    micro, levels, lat_rows, lon, width = initial_field.shape
    cells = levels * lat_rows * lon
    heads, entries = earth_bias.shape[-2:]
    slabs = lon // WW
    half_cells = cells // slabs
    hidden = expand_weight.shape[2]
    wide = -(-(width + 2) // 128) * 128
    lines = -(-heads * GROUP // 8) * 8
    tiles = cells // 16
    edges = (0, tiles // 2 * 16, (tiles - tiles // 6) * 16, cells)
    chunks = len(edges) - 1
    lanes = -(-WZ * WH * (2 * WW - 1) // 128) * 128
    q_weight, p_weight = qkv_weight[0].T, proj_weight[0].T
    vmem = pl.BlockSpec(memory_space=pltpu.VMEM)
    dma = pltpu.SemaphoreType.DMA
    out = pl.pallas_call(
        functools.partial(kernel, tp, heads, slabs, edges),
        out_shape=jax.ShapeDtypeStruct((micro, cells, width), BF16),
        in_specs=[pl.BlockSpec(memory_space=pltpu.HBM)] * 14,
        out_specs=vmem,
        scratch_shapes=[
            pltpu.VMEM((cells, width), BF16),
            pltpu.VMEM((1, width), BF16),
            pltpu.VMEM((1, width), BF16),
            pltpu.VMEM(q_weight.shape, BF16),
            pltpu.VMEM(qkv_bias.shape, BF16),
            pltpu.VMEM(p_weight.shape, BF16),
            pltpu.VMEM(proj_bias.shape, BF16),
            pltpu.VMEM((1, width), BF16),
            pltpu.VMEM((1, width), BF16),
            pltpu.VMEM((width, hidden), BF16),
            pltpu.VMEM((1, hidden), BF16),
            pltpu.VMEM(reduce_bias.shape, BF16),
            pltpu.VMEM((2, heads, 1, entries), F32),
            pltpu.VMEM((2, 3 * width, wide), BF16),
            pltpu.VMEM((2, width, wide), BF16),
            pltpu.VMEM((2, tp * hidden, wide), BF16),
            pltpu.VMEM((2, tp * hidden, width), BF16),
            pltpu.VMEM((2, 16, width), BF16),
            pltpu.VMEM((cells, width), BF16),
            pltpu.VMEM((cells, width), BF16),
            pltpu.VMEM((2, cells, width), BF16),
            pltpu.VMEM((cells, width), BF16),
            pltpu.VMEM((cells, cells), BF16),
            pltpu.VMEM((cells, cells), BF16),
            pltpu.VMEM((cells, wide), BF16),
            pltpu.VMEM((cells, wide), BF16),
            pltpu.VMEM((cells, wide), BF16),
            pltpu.VMEM((lines, lanes), F32),
            pltpu.VMEM((heads * half_cells, 2 * half_cells), F32),
            pltpu.VMEM((2 * half_cells, heads * half_cells), F32),
            dma((14,)),
            dma((2, 8, 4)),
            dma((2, 8, 4)),
            dma,
            dma,
            dma((chunks,)),
            dma((chunks,)),
            dma((chunks,)),
            dma((chunks,)),
        ],
        compiler_params=pltpu.CompilerParams(
            collective_id=0, has_side_effects=True, vmem_limit_bytes=60 * 1024 * 1024),
    )(
        initial_field.reshape(micro, cells, width), first_gain, first_shift, q_weight, qkv_bias,
        p_weight, proj_bias, second_gain, second_shift, expand_weight[0], expand_bias,
        reduce_weight[0], reduce_bias, earth_bias.reshape(heads, 1, entries),
    )
    return out.reshape(1, micro, levels, lat_rows, lon, width)


def solution(mesh):
    return jax.shard_map(
        on_device,
        mesh=mesh,
        in_specs=(
            P(None, "tp", "lat", None, None),
            P("section", None),
            P("section", None),
            P("section", None, "tp"),
            P("section", "tp"),
            P("section", None, "tp"),
            P("section", "tp"),
            P("section", None),
            P("section", None),
            P("section", None, "tp"),
            P("section", "tp"),
            P("section", "tp", None),
            P("section", "tp"),
            P("section", "tp", "lat", None, None),
        ),
        out_specs=P("section", None, "tp", "lat", None, None),
        check_vma=False,
    )
```

```python
import functools

import jax
import jax.numpy as jnp
import numpy as np
from jax import lax
from jax.experimental import pallas as pl
from jax.experimental.pallas import tpu as pltpu
from jax.sharding import PartitionSpec as P

WZ = 2
WH = 6
WW = 12
HALF = WH // 2
GROUP = WZ * HALF
EPS = 1e-05
MESH = pl.DeviceIdType.MESH
F32 = jnp.float32
BF16 = jnp.bfloat16
NT = (((1,), (1,)), ((), ()))
TN = (((0,), (0,)), ((), ()))
LOG2E = float(np.log2(np.e))


def mm(a, b):
    return jnp.dot(a, b, preferred_element_type=F32)


def mm_nt(a, b):
    return lax.dot_general(a, b, NT, preferred_element_type=F32)


def layer_norm(values, gain, shift):
    mean = jnp.mean(values, axis=-1, keepdims=True)
    centred = values - mean
    spread = jnp.mean(centred * centred, axis=-1, keepdims=True)
    return centred * lax.rsqrt(spread + EPS) * gain + shift


def kernel(
    tp, heads, slabs, all_edges,
    x_in, g1_in, s1_in, qw_in, qb_in, pw_in, pb_in, g2_in, s2_in,
    ew_in, eb_in, rw_in, rb_in, table_in,
    out_ref,
    x_ref, g1_ref, s1_ref, qw_ref, qb_ref, pw_ref, pb_ref, g2_ref, s2_ref,
    ew_ref, eb_ref, rb_ref, tables,
    first_share, second_share, reduce, near_raw, near_mid, outp, foreign, perm, unperm,
    own_n, near_n, att_n, table, spread, bias,
    l_sem, w_send, w_recv, f_send, f_recv, n_send, n_recv, o_send, o_recv,
):
    me = lax.axis_index("tp")
    lat = lax.axis_index("lat")
    section = lax.axis_index("section")
    pair = lat + 1 - 2 * lax.rem(lat, 2)
    other = 1 - section
    cells, width = x_ref.shape
    wide = own_n.shape[1]
    half_cells = cells // slabs
    head_size = width // heads
    q_part, p_part, e_part = qw_ref.shape[0], pw_ref.shape[0], ew_ref.shape[1]
    core_peer = me + 1 - 2 * lax.rem(me, 2)
    chip_peer = lax.rem(me + tp // 2, tp)

    barrier = pltpu.get_barrier_semaphore()
    pl.semaphore_signal(barrier, inc=1, device_id={"tp": core_peer}, device_id_type=MESH)
    pl.semaphore_signal(barrier, inc=1, device_id={"tp": chip_peer}, device_id_type=MESH)
    pl.semaphore_signal(barrier, inc=1, device_id={"lat": pair}, device_id_type=MESH)
    pl.semaphore_signal(barrier, inc=1, device_id={"section": other}, device_id_type=MESH)

    def owner_rows(owner, part):
        return pl.ds(pl.multiple_of(owner * part, 16), part)

    loads = [
        pltpu.make_async_copy(source, target, l_sem.at[n])
        for n, (source, target) in enumerate((
            (qw_in, qw_ref), (qb_in, qb_ref), (pw_in, pw_ref), (pb_in, pb_ref), (rb_in, rb_ref),
            (ew_in, ew_ref), (eb_in, eb_ref), (rw_in, reduce.at[section, owner_rows(me, e_part), :]),
            (g1_in, g1_ref), (s1_in, s1_ref), (g2_in, g2_ref), (s2_in, s2_ref),
            (x_in.at[section], x_ref), (table_in, tables.at[section]),
        ))
    ]
    for load in loads:
        load.start()

    for load in loads[:2] + loads[8:12]:
        load.wait()
    tail = lax.broadcasted_iota(jnp.int32, (wide - width, q_part), 0)
    q_tail = jnp.where(tail == 0, qb_ref[...].astype(F32), 0.0).T
    first_share[section, me, :q_part, :] = jnp.concatenate(
        [qw_ref[...].astype(F32), q_tail], axis=1).astype(BF16)
    line = lax.broadcasted_iota(jnp.int32, (16, width), 0)
    packed = jnp.where(line == 0, g1_ref[...].astype(F32), s1_ref[...].astype(F32))
    packed = jnp.where(line == 2, g2_ref[...].astype(F32), packed)
    first_share[section, me, q_part:, :width] = jnp.where(line == 3, s2_ref[...].astype(F32), packed).astype(BF16)

    pl.semaphore_wait(barrier, 4)

    def weight_copy(model, kind, way):
        owner = chip_peer if way == 2 else me
        target = (
            lambda: first_share.at[model, owner],
            lambda: second_share.at[model, owner],
            lambda: reduce.at[model, owner_rows(owner, e_part), :],
            lambda: tables.at[model],
        )[kind]()
        device = ({"tp": core_peer}, {"tp": chip_peer}, {"tp": core_peer}, {"section": other})[way]
        return pltpu.make_async_remote_copy(
            src_ref=table_in if kind == 3 else target, dst_ref=target,
            send_sem=w_send.at[model, kind, way], recv_sem=w_recv.at[model, kind, way],
            device_id=device, device_id_type=MESH)

    def share_out(model, kind):
        @pl.when(section != model)
        def _():
            weight_copy(model, kind, 3).wait_recv()

        weight_copy(model, kind, 1).start()
        weight_copy(model, kind, 0).start()

    def hand_on(model, kind):
        weight_copy(model, kind, 1).wait_recv()
        weight_copy(model, kind, 2).start()

    def weights_here(model, kind):
        weight_copy(model, kind, 0).wait_recv()
        weight_copy(model, kind, 2).wait_recv()

    field_copy = pltpu.make_async_remote_copy(
        src_ref=x_in.at[section], dst_ref=near_raw, send_sem=f_send, recv_sem=f_recv,
        device_id={"lat": pair}, device_id_type=MESH)
    edges, all_rows = all_edges
    chunks = len(edges) - 1

    def pair_copy(part):
        rows = pl.ds(edges[part], edges[part + 1] - edges[part])
        return pltpu.make_async_remote_copy(
            src_ref=outp.at[0, rows], dst_ref=near_mid.at[rows], send_sem=n_send.at[part],
            recv_sem=n_recv.at[part], device_id={"lat": pair}, device_id_type=MESH)

    def result_copy(model):
        return pltpu.make_async_remote_copy(
            src_ref=outp.at[model], dst_ref=foreign, send_sem=o_send, recv_sem=o_recv,
            device_id={"section": other}, device_id_type=MESH)

    def own_shares(*kinds):
        for kind in kinds:
            weight_copy(section, kind, 3).start()

        @pl.when(section == 0)
        def _():
            for kind in kinds:
                if kind < 3:
                    weight_copy(0, kind, 1).start()
                    weight_copy(0, kind, 0).start()

    own_shares(0, 3)
    field_copy.start()
    for load in loads[2:8]:
        load.wait()
    tail = lax.broadcasted_iota(jnp.int32, (wide - width, p_part), 0)
    p_tail = jnp.where(
        tail == 0, pb_ref[...].astype(F32), jnp.where(tail == 1, rb_ref[...].astype(F32), 0.0)).T
    second_share[section, me, e_part:, :] = jnp.concatenate(
        [pw_ref[...].astype(F32), p_tail], axis=1).astype(BF16)
    tail = lax.broadcasted_iota(jnp.int32, (wide - width, e_part), 0)
    second_share[section, me, :e_part, :] = jnp.concatenate(
        [ew_ref[...].astype(F32), jnp.where(tail == 0, eb_ref[...].astype(F32), 0.0)], axis=0).T.astype(BF16)
    own_shares(1, 2)

    def share_on(kind):
        @pl.when(section == 1)
        def _():
            weight_copy(0, kind, 3).wait_recv()
            weight_copy(0, kind, 1).start()
            weight_copy(0, kind, 0).start()

    for load in loads[12:]:
        load.wait()

    stretch = cells // GROUP
    step = -(-65536 // GROUP)
    line = lax.broadcasted_iota(jnp.int32, (1, cells), 1)
    level_row = sum((line >= stretch * k).astype(jnp.int32) for k in range(1, GROUP))
    forth = (line - stretch * level_row) * GROUP + level_row
    column = lax.shift_right_logical(line * step, 16)
    back = (line - GROUP * column) * stretch + column
    rows = lax.broadcasted_iota(jnp.int32, (cells, cells), 0)
    perm[...] = (rows == forth).astype(F32).astype(BF16)
    unperm[...] = (rows == back).astype(F32).astype(BF16)
    lanes = lax.broadcasted_iota(jnp.int32, (cells, wide), 1)
    ones = (lanes == width).astype(F32).astype(BF16)
    own_n[...] = ones
    near_n[...] = ones
    att_n[...] = ones
    own_field = mm(perm[...], x_ref[...])

    span = WH * (2 * WW - 1)
    c = lax.broadcasted_iota(jnp.int32, (1, 2 * half_cells), 1)
    far = (c >= half_cells).astype(jnp.int32)
    c = c - half_cells * far
    wk = sum((c >= GROUP * k).astype(jnp.int32) for k in range(1, WW))
    zr = c - GROUP * wk
    zk = (zr >= HALF).astype(jnp.int32)
    band = lax.rem(lat, 2)
    hk = zr - HALF * zk + HALF * (band + far - 2 * band * far)
    place = zk * span + hk * (2 * WW - 1) + WW - 1 - wk
    pick = (lax.broadcasted_iota(jnp.int32, (table.shape[1], 2 * half_cells), 0) == place).astype(F32).astype(BF16)
    table[...] = jnp.zeros_like(table)

    def expand_bias(model):
        for zq in range(WZ):
            for zk in range(WZ):
                for r in range(HALF):
                    off = ((zq * WZ + zk) * HALF + r) * span
                    piece = tables[model, :, 0, off:off + span]
                    for h in range(heads):
                        row = h * GROUP + zq * HALF + r
                        table[row:row + 1, zk * span:(zk + 1) * span] = piece[h:h + 1]
        full = table[...]
        lines = full.shape[0]
        turned = jnp.concatenate(
            [full if wq == 0 else pltpu.roll(full, full.shape[1] - wq, 1) for wq in range(WW)], axis=0)
        first = turned.astype(BF16)
        rest = turned - first.astype(F32)
        second = rest.astype(BF16)
        third = (rest - second.astype(F32)).astype(BF16)
        hand_on(model, 0)
        total = mm(first, pick) + mm(second, pick) + mm(third, pick)
        for wq in range(WW):
            for h in range(heads):
                at, row = h * half_cells + wq * GROUP, wq * lines + h * GROUP
                spread[at:at + GROUP, :] = total[row:row + GROUP]
        bias[...] = spread[...].T * LOG2E

    share_on(0)

    scale = LOG2E / float(np.sqrt(head_size))
    lane_head = lax.broadcasted_iota(jnp.int32, (half_cells, width), 1)
    in_head = [(lane_head >= h * head_size) & (lane_head < (h + 1) * head_size) for h in range(heads)]

    for model in range(2):
        @pl.when(section != model)
        def _():
            weight_copy(model, 3, 3).wait_recv()

        expand_bias(model)
        if model == 0:
            share_on(1)
        norms = first_share[model, me, q_part:, :width].astype(F32)
        g1, s1, g2, s2 = (norms[n:n + 1] for n in range(4))
        grid = own_field if model == 0 else outp[0].astype(F32)
        own_n[:, :width] = layer_norm(grid, g1, s1).astype(BF16)
        weights_here(model, 0)
        qkv = first_share[model, :, :q_part, :].reshape(3 * width, wide)
        q = mm_nt(own_n[...], qkv[:width])
        k_own = mm_nt(own_n[...], qkv[width:2 * width])
        v_own = mm_nt(own_n[...], qkv[2 * width:])
        if model == 0:
            field_copy.wait_recv()
            near = mm(perm[...], near_raw[...])
        else:
            for part in range(chunks):
                pair_copy(part).wait_recv()
            near = near_mid[...].astype(F32)
        near_n[:, :width] = layer_norm(near, g1, s1).astype(BF16)
        k_near = mm_nt(near_n[...], qkv[width:2 * width])
        v_near = mm_nt(near_n[...], qkv[2 * width:])
        if model == 0:
            share_on(2)
        attended = []
        for s in range(slabs):
            cut = slice(s * half_cells, (s + 1) * half_cells)
            keys = jnp.concatenate([k_own[cut], k_near[cut]], axis=0).astype(BF16)
            vals = jnp.concatenate([v_own[cut], v_near[cut]], axis=0).astype(BF16)
            stack = jnp.concatenate([jnp.where(m, q[cut], 0.0) for m in in_head], axis=0).astype(BF16)
            scores = mm_nt(keys, stack) * scale + bias[...]
            e = jnp.exp2(scores - jnp.max(scores, axis=0, keepdims=True))
            probs = (e * (1.0 / jnp.sum(e, axis=0, keepdims=True))).astype(BF16)
            mixed = lax.dot_general(probs, vals, TN, preferred_element_type=F32)
            total = jnp.zeros((half_cells, width), F32)
            for h, m in enumerate(in_head):
                total = jnp.where(m, mixed[h * half_cells:(h + 1) * half_cells], total)
            attended.append(total)
        att_n[:, :width] = jnp.concatenate(attended, axis=0).astype(BF16)
        hand_on(model, 1)
        weights_here(model, 1)
        proj = second_share[model, :, e_part:, :].reshape(width, wide)
        expand = second_share[model, :, :e_part, :].reshape(tp * e_part, wide)
        middle = (grid + mm_nt(att_n[...], proj)).astype(BF16).astype(F32)
        pick_row = (lax.broadcasted_iota(jnp.int32, (16, wide), 1) == width + 1).astype(F32).astype(BF16)
        shift_out = mm_nt(pick_row, proj)[:1]
        own_n[:, :width] = layer_norm(middle, g2, s2).astype(BF16)
        hand_on(model, 2)
        if model == 0:
            for kind in range(3):
                share_out(1, kind)
        own_edges = all_edges[model]
        for part in range(len(own_edges) - 1):
            cut = slice(own_edges[part], own_edges[part + 1])
            pre = mm_nt(own_n[cut, :], expand)
            hidden = (0.5 * pre * (1.0 + lax.erf(pre * float(np.sqrt(0.5))))).astype(BF16)
            if part == 0:
                weights_here(model, 2)
            result = middle[cut] + shift_out + mm(hidden, reduce[model])
            outp[model, cut, :] = result.astype(BF16)
            if model == 0:
                pair_copy(part).start()

        @pl.when(section != model)
        def _():
            result_copy(model).start()

    @pl.when(section == 0)
    def _():
        out_ref[0] = mm(unperm[...], outp[0]).astype(BF16)

    @pl.when(section == 1)
    def _():
        out_ref[1] = mm(unperm[...], outp[1]).astype(BF16)

    result_copy(other).wait_recv()
    out_ref[other] = mm(unperm[...], foreign[...]).astype(BF16)

    for kind in range(4):
        weight_copy(section, kind, 3).wait_send()
    for model in range(2):
        for kind in range(3):
            for way in range(3):
                weight_copy(model, kind, way).wait_send()
    field_copy.wait_send()
    for part in range(chunks):
        pair_copy(part).wait_send()
    result_copy(other).wait_send()


def on_device(
    initial_field, first_gain, first_shift, qkv_weight, qkv_bias, proj_weight, proj_bias,
    second_gain, second_shift, expand_weight, expand_bias, reduce_weight, reduce_bias, earth_bias,
):
    tp = lax.axis_size("tp")
    micro, levels, lat_rows, lon, width = initial_field.shape
    cells = levels * lat_rows * lon
    heads, entries = earth_bias.shape[-2:]
    slabs = lon // WW
    half_cells = cells // slabs
    hidden = expand_weight.shape[2]
    wide = -(-(width + 2) // 128) * 128
    lines = -(-heads * GROUP // 8) * 8
    tiles = cells // 16
    edges = (0, tiles * 2 // 3 * 16, cells)
    chunks = len(edges) - 1
    lanes = -(-WZ * WH * (2 * WW - 1) // 128) * 128
    q_weight, p_weight = qkv_weight[0].T, proj_weight[0].T
    vmem = pl.BlockSpec(memory_space=pltpu.VMEM)
    dma = pltpu.SemaphoreType.DMA
    out = pl.pallas_call(
        functools.partial(kernel, tp, heads, slabs, (edges, (0, cells))),
        out_shape=jax.ShapeDtypeStruct((micro, cells, width), BF16),
        in_specs=[pl.BlockSpec(memory_space=pltpu.HBM)] * 14,
        out_specs=vmem,
        scratch_shapes=[
            pltpu.VMEM((cells, width), BF16),
            pltpu.VMEM((1, width), BF16),
            pltpu.VMEM((1, width), BF16),
            pltpu.VMEM(q_weight.shape, BF16),
            pltpu.VMEM(qkv_bias.shape, BF16),
            pltpu.VMEM(p_weight.shape, BF16),
            pltpu.VMEM(proj_bias.shape, BF16),
            pltpu.VMEM((1, width), BF16),
            pltpu.VMEM((1, width), BF16),
            pltpu.VMEM((width, hidden), BF16),
            pltpu.VMEM((1, hidden), BF16),
            pltpu.VMEM(reduce_bias.shape, BF16),
            pltpu.VMEM((2, heads, 1, entries), F32),
            pltpu.VMEM((2, tp, q_weight.shape[0] + 16, wide), BF16),
            pltpu.VMEM((2, tp, hidden + p_weight.shape[0], wide), BF16),
            pltpu.VMEM((2, tp * hidden, width), BF16),
            pltpu.VMEM((cells, width), BF16),
            pltpu.VMEM((cells, width), BF16),
            pltpu.VMEM((2, cells, width), BF16),
            pltpu.VMEM((cells, width), BF16),
            pltpu.VMEM((cells, cells), BF16),
            pltpu.VMEM((cells, cells), BF16),
            pltpu.VMEM((cells, wide), BF16),
            pltpu.VMEM((cells, wide), BF16),
            pltpu.VMEM((cells, wide), BF16),
            pltpu.VMEM((lines, lanes), F32),
            pltpu.VMEM((heads * half_cells, 2 * half_cells), F32),
            pltpu.VMEM((2 * half_cells, heads * half_cells), F32),
            dma((14,)),
            dma((2, 4, 4)),
            dma((2, 4, 4)),
            dma,
            dma,
            dma((chunks,)),
            dma((chunks,)),
            dma,
            dma,
        ],
        compiler_params=pltpu.CompilerParams(
            collective_id=0, has_side_effects=True, vmem_limit_bytes=60 * 1024 * 1024),
    )(
        initial_field.reshape(micro, cells, width), first_gain, first_shift, q_weight, qkv_bias,
        p_weight, proj_bias, second_gain, second_shift, expand_weight[0], expand_bias,
        reduce_weight[0], reduce_bias, earth_bias.reshape(heads, 1, entries),
    )
    return out.reshape(1, micro, levels, lat_rows, lon, width)


def solution(mesh):
    return jax.shard_map(
        on_device,
        mesh=mesh,
        in_specs=(
            P(None, "tp", "lat", None, None),
            P("section", None),
            P("section", None),
            P("section", None, "tp"),
            P("section", "tp"),
            P("section", None, "tp"),
            P("section", "tp"),
            P("section", None),
            P("section", None),
            P("section", None, "tp"),
            P("section", "tp"),
            P("section", "tp", None),
            P("section", "tp"),
            P("section", "tp", "lat", None, None),
        ),
        out_specs=P("section", None, "tp", "lat", None, None),
        check_vma=False,
    )
```

```python
import functools

import jax
import jax.numpy as jnp
import numpy as np
from jax import lax
from jax.experimental import pallas as pl
from jax.experimental.pallas import tpu as pltpu
from jax.sharding import PartitionSpec as P

WZ = 2
WH = 6
WW = 12
HALF = WH // 2
GROUP = WZ * HALF
EPS = 1e-05
MESH = pl.DeviceIdType.MESH
F32 = jnp.float32
BF16 = jnp.bfloat16
NT = (((1,), (1,)), ((), ()))
TN = (((0,), (0,)), ((), ()))
LOG2E = float(np.log2(np.e))


def mm(a, b):
    return jnp.dot(a, b, preferred_element_type=F32)


def mm_nt(a, b):
    return lax.dot_general(a, b, NT, preferred_element_type=F32)


def layer_norm(values, gain, shift):
    mean = jnp.mean(values, axis=-1, keepdims=True)
    centred = values - mean
    spread = jnp.mean(centred * centred, axis=-1, keepdims=True)
    return centred * lax.rsqrt(spread + EPS) * gain + shift


def kernel(
    tp, heads, slabs, edges,
    x_in, g1_in, s1_in, qw_in, qb_in, pw_in, pb_in, g2_in, s2_in,
    ew_in, eb_in, rw_in, rb_in, table_in,
    out_ref,
    x_ref, g1_ref, s1_ref, qw_ref, qb_ref, pw_ref, pb_ref, g2_ref, s2_ref,
    ew_ref, eb_ref, rb_ref, tables,
    qkv, proj, expand, reduce, norms, near_raw, near_mid, outp, foreign, perm, unperm,
    own_n, near_n, att_n, table, spread, bias,
    l_sem, w_send, w_recv, f_send, f_recv, n_send, n_recv, o_send, o_recv,
):
    me = lax.axis_index("tp")
    lat = lax.axis_index("lat")
    section = lax.axis_index("section")
    pair = lat + 1 - 2 * lax.rem(lat, 2)
    other = 1 - section
    cells, width = x_ref.shape
    wide = own_n.shape[1]
    half_cells = cells // slabs
    head_size = width // heads
    q_part, p_part, e_part = qw_ref.shape[0], pw_ref.shape[0], ew_ref.shape[1]
    core_peer = me + 1 - 2 * lax.rem(me, 2)
    chip_peer = lax.rem(me + tp // 2, tp)

    barrier = pltpu.get_barrier_semaphore()
    pl.semaphore_signal(barrier, inc=1, device_id={"tp": core_peer}, device_id_type=MESH)
    pl.semaphore_signal(barrier, inc=1, device_id={"tp": chip_peer}, device_id_type=MESH)
    pl.semaphore_signal(barrier, inc=1, device_id={"lat": pair}, device_id_type=MESH)
    pl.semaphore_signal(barrier, inc=1, device_id={"section": other}, device_id_type=MESH)

    def owner_rows(owner, part):
        return pl.ds(pl.multiple_of(owner * part, 16), part)

    loads = [
        pltpu.make_async_copy(source, target, l_sem.at[n])
        for n, (source, target) in enumerate((
            (qw_in, qw_ref), (qb_in, qb_ref), (pw_in, pw_ref), (pb_in, pb_ref), (rb_in, rb_ref),
            (ew_in, ew_ref), (eb_in, eb_ref), (rw_in, reduce.at[section, owner_rows(me, e_part), :]),
            (g1_in, g1_ref), (s1_in, s1_ref), (g2_in, g2_ref), (s2_in, s2_ref),
            (x_in.at[section], x_ref), (table_in, tables.at[section]),
        ))
    ]
    for load in loads:
        load.start()

    for load in loads[:5]:
        load.wait()
    tail = lax.broadcasted_iota(jnp.int32, (wide - width, q_part), 0)
    q_tail = jnp.where(tail == 0, qb_ref[...].astype(F32), 0.0).T
    qkv[section, owner_rows(me, q_part), :] = jnp.concatenate(
        [qw_ref[...].astype(F32), q_tail], axis=1).astype(BF16)
    tail = lax.broadcasted_iota(jnp.int32, (wide - width, p_part), 0)
    p_tail = jnp.where(
        tail == 0, pb_ref[...].astype(F32), jnp.where(tail == 1, rb_ref[...].astype(F32), 0.0)).T
    proj[section, owner_rows(me, p_part), :] = jnp.concatenate(
        [pw_ref[...].astype(F32), p_tail], axis=1).astype(BF16)
    for load in loads[5:12]:
        load.wait()
    tail = lax.broadcasted_iota(jnp.int32, (wide - width, e_part), 0)
    expand[section, owner_rows(me, e_part), :] = jnp.concatenate(
        [ew_ref[...].astype(F32), jnp.where(tail == 0, eb_ref[...].astype(F32), 0.0)], axis=0).T.astype(BF16)
    line = lax.broadcasted_iota(jnp.int32, (16, width), 0)
    packed = jnp.where(line == 0, g1_ref[...].astype(F32), s1_ref[...].astype(F32))
    packed = jnp.where(line == 2, g2_ref[...].astype(F32), packed)
    norms[section] = jnp.where(line == 3, s2_ref[...].astype(F32), packed).astype(BF16)

    pl.semaphore_wait(barrier, 4)

    def weight_copy(model, kind, way):
        owner = chip_peer if way == 2 else me
        target = (
            lambda: qkv.at[model, owner_rows(owner, q_part), :],
            lambda: proj.at[model, owner_rows(owner, p_part), :],
            lambda: expand.at[model, owner_rows(owner, e_part), :],
            lambda: reduce.at[model, owner_rows(owner, e_part), :],
            lambda: norms.at[model],
            lambda: tables.at[model],
        )[kind]()
        device = ({"tp": core_peer}, {"tp": chip_peer}, {"tp": core_peer}, {"section": other})[way]
        return pltpu.make_async_remote_copy(
            src_ref=table_in if kind == 5 else target, dst_ref=target,
            send_sem=w_send.at[model, kind, way], recv_sem=w_recv.at[model, kind, way],
            device_id=device, device_id_type=MESH)

    def share_out(model, kind):
        @pl.when(section != model)
        def _():
            weight_copy(model, kind, 3).wait_recv()

        weight_copy(model, kind, 1).start()
        weight_copy(model, kind, 0).start()

    def hand_on(model, kind):
        weight_copy(model, kind, 1).wait_recv()
        weight_copy(model, kind, 2).start()

    def weights_here(model, kind):
        weight_copy(model, kind, 0).wait_recv()
        weight_copy(model, kind, 2).wait_recv()

    field_copy = pltpu.make_async_remote_copy(
        src_ref=x_in.at[section], dst_ref=near_raw, send_sem=f_send, recv_sem=f_recv,
        device_id={"lat": pair}, device_id_type=MESH)
    chunks = len(edges) - 1

    def pair_copy(part):
        rows = pl.ds(edges[part], edges[part + 1] - edges[part])
        return pltpu.make_async_remote_copy(
            src_ref=outp.at[0, rows], dst_ref=near_mid.at[rows], send_sem=n_send.at[part],
            recv_sem=n_recv.at[part], device_id={"lat": pair}, device_id_type=MESH)

    def result_copy(model, part):
        rows = pl.ds(edges[part], edges[part + 1] - edges[part])
        return pltpu.make_async_remote_copy(
            src_ref=outp.at[model, rows], dst_ref=foreign.at[rows], send_sem=o_send.at[part],
            recv_sem=o_recv.at[part], device_id={"section": other}, device_id_type=MESH)

    weight_copy(section, 0, 3).start()

    @pl.when(section == 0)
    def _():
        weight_copy(0, 0, 1).start()
        weight_copy(0, 0, 0).start()

    field_copy.start()
    for kind in (5, 4, 1, 2, 3):
        weight_copy(section, kind, 3).start()

    @pl.when(section == 0)
    def _():
        for kind in (1, 2, 3):
            weight_copy(0, kind, 1).start()
            weight_copy(0, kind, 0).start()

    def share_on(kind):
        @pl.when(section == 1)
        def _():
            weight_copy(0, kind, 3).wait_recv()
            weight_copy(0, kind, 1).start()
            weight_copy(0, kind, 0).start()

    for load in loads[12:]:
        load.wait()

    stretch = cells // GROUP
    step = -(-65536 // GROUP)
    line = lax.broadcasted_iota(jnp.int32, (1, cells), 1)
    level_row = sum((line >= stretch * k).astype(jnp.int32) for k in range(1, GROUP))
    forth = (line - stretch * level_row) * GROUP + level_row
    column = lax.shift_right_logical(line * step, 16)
    back = (line - GROUP * column) * stretch + column
    rows = lax.broadcasted_iota(jnp.int32, (cells, cells), 0)
    perm[...] = (rows == forth).astype(F32).astype(BF16)
    unperm[...] = (rows == back).astype(F32).astype(BF16)
    lanes = lax.broadcasted_iota(jnp.int32, (cells, wide), 1)
    ones = (lanes == width).astype(F32).astype(BF16)
    own_n[...] = ones
    near_n[...] = ones
    att_n[...] = ones
    own_field = mm(perm[...], x_ref[...])

    span = WH * (2 * WW - 1)
    c = lax.broadcasted_iota(jnp.int32, (1, 2 * half_cells), 1)
    far = (c >= half_cells).astype(jnp.int32)
    c = c - half_cells * far
    wk = sum((c >= GROUP * k).astype(jnp.int32) for k in range(1, WW))
    zr = c - GROUP * wk
    zk = (zr >= HALF).astype(jnp.int32)
    band = lax.rem(lat, 2)
    hk = zr - HALF * zk + HALF * (band + far - 2 * band * far)
    place = zk * span + hk * (2 * WW - 1) + WW - 1 - wk
    pick = (lax.broadcasted_iota(jnp.int32, (table.shape[1], 2 * half_cells), 0) == place).astype(F32).astype(BF16)
    table[...] = jnp.zeros_like(table)

    def expand_bias(model):
        for zq in range(WZ):
            for zk in range(WZ):
                for r in range(HALF):
                    off = ((zq * WZ + zk) * HALF + r) * span
                    piece = tables[model, :, 0, off:off + span]
                    for h in range(heads):
                        row = h * GROUP + zq * HALF + r
                        table[row:row + 1, zk * span:(zk + 1) * span] = piece[h:h + 1]
        full = table[...]
        lines = full.shape[0]
        turned = jnp.concatenate(
            [full if wq == 0 else pltpu.roll(full, full.shape[1] - wq, 1) for wq in range(WW)], axis=0)
        first = turned.astype(BF16)
        rest = turned - first.astype(F32)
        second = rest.astype(BF16)
        third = (rest - second.astype(F32)).astype(BF16)
        total = mm(first, pick) + mm(second, pick) + mm(third, pick)
        for wq in range(WW):
            for h in range(heads):
                at, row = h * half_cells + wq * GROUP, wq * lines + h * GROUP
                spread[at:at + GROUP, :] = total[row:row + GROUP]
        bias[...] = spread[...].T * LOG2E

    share_on(0)
    share_on(1)

    scale = LOG2E / float(np.sqrt(head_size))
    lane_head = lax.broadcasted_iota(jnp.int32, (half_cells, width), 1)
    in_head = [(lane_head >= h * head_size) & (lane_head < (h + 1) * head_size) for h in range(heads)]

    for model in range(2):
        @pl.when(section != model)
        def _():
            weight_copy(model, 4, 3).wait_recv()
            weight_copy(model, 5, 3).wait_recv()

        expand_bias(model)
        g1, s1, g2, s2 = (norms[model, n:n + 1, :].astype(F32) for n in range(4))
        hand_on(model, 0)
        grid = own_field if model == 0 else outp[0].astype(F32)
        own_n[:, :width] = layer_norm(grid, g1, s1).astype(BF16)
        if model == 0:
            share_on(2)
        hand_on(model, 1)
        weights_here(model, 0)
        q = mm_nt(own_n[...], qkv[model, :width, :])
        k_own = mm_nt(own_n[...], qkv[model, width:2 * width, :])
        v_own = mm_nt(own_n[...], qkv[model, 2 * width:, :])
        if model == 0:
            field_copy.wait_recv()
            near = mm(perm[...], near_raw[...])
        else:
            for part in range(chunks):
                pair_copy(part).wait_recv()
            near = near_mid[...].astype(F32)
        near_n[:, :width] = layer_norm(near, g1, s1).astype(BF16)
        k_near = mm_nt(near_n[...], qkv[model, width:2 * width, :])
        v_near = mm_nt(near_n[...], qkv[model, 2 * width:, :])
        if model == 0:
            share_on(3)
        else:
            hand_on(1, 2)
            hand_on(1, 3)
        attended = []
        for s in range(slabs):
            cut = slice(s * half_cells, (s + 1) * half_cells)
            keys = jnp.concatenate([k_own[cut], k_near[cut]], axis=0).astype(BF16)
            vals = jnp.concatenate([v_own[cut], v_near[cut]], axis=0).astype(BF16)
            stack = jnp.concatenate([jnp.where(m, q[cut], 0.0) for m in in_head], axis=0).astype(BF16)
            scores = mm_nt(keys, stack) * scale + bias[...]
            e = jnp.exp2(scores - jnp.max(scores, axis=0, keepdims=True))
            probs = (e * (1.0 / jnp.sum(e, axis=0, keepdims=True))).astype(BF16)
            mixed = lax.dot_general(probs, vals, TN, preferred_element_type=F32)
            total = jnp.zeros((half_cells, width), F32)
            for h, m in enumerate(in_head):
                total = jnp.where(m, mixed[h * half_cells:(h + 1) * half_cells], total)
            attended.append(total)
            if model == 0 and s == slabs - 2:
                hand_on(0, 2)
        att_n[:, :width] = jnp.concatenate(attended, axis=0).astype(BF16)
        if model == 0:
            hand_on(0, 3)
        weights_here(model, 1)
        middle = (grid + mm_nt(att_n[...], proj[model])).astype(BF16).astype(F32)
        pick_row = (lax.broadcasted_iota(jnp.int32, (16, wide), 1) == width + 1).astype(F32).astype(BF16)
        shift_out = mm_nt(pick_row, proj[model])[:1]
        own_n[:, :width] = layer_norm(middle, g2, s2).astype(BF16)
        if model == 0:
            for kind in range(4):
                share_out(1, kind)
        weights_here(model, 2)
        for part in range(chunks):
            cut = slice(edges[part], edges[part + 1])
            pre = mm_nt(own_n[cut, :], expand[model])
            hidden = (0.5 * pre * (1.0 + lax.erf(pre * float(np.sqrt(0.5))))).astype(BF16)
            if part == 0:
                weights_here(model, 3)
            result = middle[cut] + shift_out + mm(hidden, reduce[model])
            outp[model, cut, :] = result.astype(BF16)
            if model == 0:
                pair_copy(part).start()

            @pl.when(section != model)
            def _():
                result_copy(model, part).start()

    @pl.when(section == 0)
    def _():
        out_ref[0] = mm(unperm[...], outp[0]).astype(BF16)

    @pl.when(section == 1)
    def _():
        out_ref[1] = mm(unperm[...], outp[1]).astype(BF16)

    for part in range(chunks):
        result_copy(other, part).wait_recv()
    out_ref[other] = mm(unperm[...], foreign[...]).astype(BF16)

    for kind in range(6):
        weight_copy(section, kind, 3).wait_send()
    for model in range(2):
        for kind in range(4):
            for way in range(3):
                weight_copy(model, kind, way).wait_send()
    field_copy.wait_send()
    for part in range(chunks):
        pair_copy(part).wait_send()
        result_copy(other, part).wait_send()


def on_device(
    initial_field, first_gain, first_shift, qkv_weight, qkv_bias, proj_weight, proj_bias,
    second_gain, second_shift, expand_weight, expand_bias, reduce_weight, reduce_bias, earth_bias,
):
    tp = lax.axis_size("tp")
    micro, levels, lat_rows, lon, width = initial_field.shape
    cells = levels * lat_rows * lon
    heads, entries = earth_bias.shape[-2:]
    slabs = lon // WW
    half_cells = cells // slabs
    hidden = expand_weight.shape[2]
    wide = -(-(width + 2) // 128) * 128
    lines = -(-heads * GROUP // 8) * 8
    tiles = cells // 16
    edges = (0, tiles // 2 * 16, (tiles - tiles // 6) * 16, cells)
    chunks = len(edges) - 1
    lanes = -(-WZ * WH * (2 * WW - 1) // 128) * 128
    q_weight, p_weight = qkv_weight[0].T, proj_weight[0].T
    vmem = pl.BlockSpec(memory_space=pltpu.VMEM)
    dma = pltpu.SemaphoreType.DMA
    out = pl.pallas_call(
        functools.partial(kernel, tp, heads, slabs, edges),
        out_shape=jax.ShapeDtypeStruct((micro, cells, width), BF16),
        in_specs=[pl.BlockSpec(memory_space=pltpu.HBM)] * 14,
        out_specs=vmem,
        scratch_shapes=[
            pltpu.VMEM((cells, width), BF16),
            pltpu.VMEM((1, width), BF16),
            pltpu.VMEM((1, width), BF16),
            pltpu.VMEM(q_weight.shape, BF16),
            pltpu.VMEM(qkv_bias.shape, BF16),
            pltpu.VMEM(p_weight.shape, BF16),
            pltpu.VMEM(proj_bias.shape, BF16),
            pltpu.VMEM((1, width), BF16),
            pltpu.VMEM((1, width), BF16),
            pltpu.VMEM((width, hidden), BF16),
            pltpu.VMEM((1, hidden), BF16),
            pltpu.VMEM(reduce_bias.shape, BF16),
            pltpu.VMEM((2, heads, 1, entries), F32),
            pltpu.VMEM((2, 3 * width, wide), BF16),
            pltpu.VMEM((2, width, wide), BF16),
            pltpu.VMEM((2, tp * hidden, wide), BF16),
            pltpu.VMEM((2, tp * hidden, width), BF16),
            pltpu.VMEM((2, 16, width), BF16),
            pltpu.VMEM((cells, width), BF16),
            pltpu.VMEM((cells, width), BF16),
            pltpu.VMEM((2, cells, width), BF16),
            pltpu.VMEM((cells, width), BF16),
            pltpu.VMEM((cells, cells), BF16),
            pltpu.VMEM((cells, cells), BF16),
            pltpu.VMEM((cells, wide), BF16),
            pltpu.VMEM((cells, wide), BF16),
            pltpu.VMEM((cells, wide), BF16),
            pltpu.VMEM((lines, lanes), F32),
            pltpu.VMEM((heads * half_cells, 2 * half_cells), F32),
            pltpu.VMEM((2 * half_cells, heads * half_cells), F32),
            dma((14,)),
            dma((2, 6, 4)),
            dma((2, 6, 4)),
            dma,
            dma,
            dma((chunks,)),
            dma((chunks,)),
            dma((chunks,)),
            dma((chunks,)),
        ],
        compiler_params=pltpu.CompilerParams(
            collective_id=0, has_side_effects=True, vmem_limit_bytes=60 * 1024 * 1024),
    )(
        initial_field.reshape(micro, cells, width), first_gain, first_shift, q_weight, qkv_bias,
        p_weight, proj_bias, second_gain, second_shift, expand_weight[0], expand_bias,
        reduce_weight[0], reduce_bias, earth_bias.reshape(heads, 1, entries),
    )
    return out.reshape(1, micro, levels, lat_rows, lon, width)


def solution(mesh):
    return jax.shard_map(
        on_device,
        mesh=mesh,
        in_specs=(
            P(None, "tp", "lat", None, None),
            P("section", None),
            P("section", None),
            P("section", None, "tp"),
            P("section", "tp"),
            P("section", None, "tp"),
            P("section", "tp"),
            P("section", None),
            P("section", None),
            P("section", None, "tp"),
            P("section", "tp"),
            P("section", "tp", None),
            P("section", "tp"),
            P("section", "tp", "lat", None, None),
        ),
        out_specs=P("section", None, "tp", "lat", None, None),
        check_vma=False,
    )
```
